128 devices in a mesh: seq: 16 (over y, x), tp: 8 (over z, core).
Axes of the slice: x: 4, y: 4, z: 4, core: 2. Of those that a mesh axis runs over, the one named last changes fastest.
Arguments:
- hidden: bfloat16 [16384, 4096], P('seq'), may hold values from -6 to 6
- query_weight: bfloat16 [4096, 4096], P(None, 'tp'), may hold values from -0.09375 to 0.09375
- out_weight: bfloat16 [4096, 4096], P('tp'), may hold values from -0.75 to 0.75
- kv_cache: bfloat16 [128, 2, 128, 4096], P('seq', None, None, 'tp'), may hold values from -520 to 520
- nbr_shard: int32 [256, 2], P('seq'), may hold values from 0 to 15, all different within a row; in each aligned block of 16 rows (0 to 15, 16 to 31, ...) at most 4 rows name the same one
- nbr_row: int32 [256, 2], P('seq'), may hold values from 0 to 7
- nbr_count: int32 [256], P('seq'), may hold values from 1 to 2
Outputs:
- cca_out: bfloat16 [16384, 4096], P(('seq', 'tp'))
The draws below stay inside these ranges and needn't reach their ends.
Inputs may be any that keep to these rules, and one draw needn't show every extreme that they name: `nbr_shard`: in each aligned block of 16 spans (the spans of one index of seq) no shard is named more than 4 times, and the 2 neighbours of a span lie on different shards.
All inputs are finite; a program needn't handle non-finite values.
Results may differ from the reference program's by a relative error of at most 0.02.
Values may be sent and summed in bfloat16 or wider, within the bound.
A program may use at most 192 MiB of HBM per device.

```python
import math
import jax
import jax.numpy as jnp
import numpy as np
from jax import lax

D = 4096
HEADS = 32
HEAD = 128
SPAN = 64
NBR = 2
NBR_LEN = 128
TOK_DEV = 1024
R_DEV = 8
TOKENS = 16384
SPANS = 256
DB_ROWS = 128
CAP = 4
N_SEQ = 16
N_TP = 8


def draw_kv_cache(key, part):
    key = jax.random.fold_in(key, 11)
    first_key = jax.random.fold_in(key, 0)
    full_shape = (DB_ROWS, 2, NBR_LEN, D)
    result = jnp.clip(jax.random.normal(first_key, full_shape, jnp.float32), -6.0, 6.0)
    return result.astype(jnp.bfloat16)


def touch_ends(array, key, smallest, high):
    index_at = [jax.random.randint(jax.random.fold_in(key, axis), (), 0, length) for axis, length in enumerate(array.shape)]
    main_axis = array.shape.index(max(array.shape))
    neighbour = index_at[:main_axis] + [(index_at[main_axis] + 1) % array.shape[main_axis]] + index_at[main_axis + 1:]
    return array.at[tuple(index_at)].set(smallest).at[tuple(neighbour)].set(high)


def steps_of(rng, extent, pieces, least, high):
    loudness = 1.0
    for axis_at, blocks in pieces:
        heights = jax.random.uniform(jax.random.fold_in(jax.random.fold_in(rng, 6), axis_at), (blocks,), jnp.float32, least / len(pieces), high / len(pieces))
        loudness = loudness * jnp.repeat(jnp.exp(heights), extent[axis_at] // blocks).reshape((-1,) + (1,) * (len(extent) - 1 - axis_at))
    return loudness


def routed_block(key, own, number, rows, count, top, bound, slope):
    ranking = jax.random.permutation(key, count)
    crowded, common = shares(count, rows * top, bound, slope, True), shares(count, rows * top, bound, slope, False)
    places = jnp.arange(count)

    def named(sizes, turn):
        used = int((sizes > 0).sum())
        fixed = max(1, used // 4)
        shifted = fixed + (places - fixed + turn * (used - fixed)) % max(1, count - fixed)
        return jnp.zeros((count,), jnp.int32).at[ranking[jnp.where(places < fixed, places, shifted)]].set(jnp.asarray(sizes, jnp.int32))

    sizes = jnp.where(number % 4 == 0, named(crowded, number // 4), named(common, number - number // 4 - 1))
    mixed = jax.random.permutation(jax.random.fold_in(own, 3), count)
    donor, receiver = mixed[0:count // 2 * 2:2], mixed[1:count // 2 * 2:2]
    slack = jnp.minimum(sizes[donor] - 1, bound - sizes[receiver]) // 2
    slack = jnp.where((donor == ranking[0]) | (receiver == ranking[0]) | (sizes[receiver] == 0), 0, jnp.maximum(slack, 0))
    shifted = jax.random.randint(jax.random.fold_in(own, 4), (count // 2,), 0, 1 << 20) % (slack + 1)
    sizes = sizes.at[donor].add(-shifted).at[receiver].add(shifted)
    labels = jnp.searchsorted(jnp.cumsum(sizes), jnp.arange(rows * top), side="right").astype(jnp.int32)
    listing = labels.reshape(top, rows).T
    listing = listing[jax.random.permutation(jax.random.fold_in(own, 1), rows)]
    turn = jax.random.randint(jax.random.fold_in(own, 2), (rows, 1), 0, top)
    return jnp.take_along_axis(listing, (jnp.arange(top)[None, :] + turn) % top, axis=1)


def shares(count, total, limit, skew, full):
    loads = [(1 << 20) // math.isqrt(standing ** skew) + 1 for standing in range(1, count + 1)]
    largest = limit if full else min(limit, max(-(-total // count), total * loads[0] // sum(loads)))
    least = 1 if total - largest >= count - 1 else 0
    given, rest = [largest] + [least] * (count - 1), total - largest - least * (count - 1)
    while rest > 0:
        free = [i for i in range(1, count) if given[i] < largest] or [i for i in range(1, count) if given[i] < limit]
        mass, remaining = sum([loads[i] for i in free]), rest
        for i in free:
            more = min(limit - given[i], max(1, remaining * loads[i] // mass), rest)
            given[i] = given[i] + more
            rest = rest - more
    return np.array(given)


def normal_values(stream_key, shape, deviation, limit, cuts=(), kind=jnp.bfloat16):
    values = deviation * jax.random.normal(stream_key, shape, jnp.float32)
    if cuts:
        values = values * steps_of(stream_key, shape, cuts, -0.22, 0.18)
    return jnp.clip(values, -limit, limit).astype(kind)


def setup_inputs(seed: int = 0) -> dict:
    keys = jax.random.split(jax.random.key(seed), 8)
    hidden = normal_values(keys[0], (TOKENS, D), 1.0, 6.0, ((0, 16),))
    query_weight = normal_values(keys[1], (D, D), D ** -0.5, 0.09375, ((1, 8),))
    out_weight = normal_values(keys[2], (D, D), (D // 64) ** -0.5, 0.75, ((0, 8),))
    kv_cache = draw_kv_cache(jax.random.fold_in(keys[7], 71), 0)
    nbr_shard_keys = jax.random.split(jax.random.fold_in(keys[4], 1), SPANS // (TOK_DEV // SPAN))
    nbr_shard_turns = jax.random.permutation(jax.random.fold_in(keys[4], 3), SPANS // (TOK_DEV // SPAN))
    nbr_shard = jax.vmap(lambda own, number: routed_block(jax.random.fold_in(keys[4], 2), own, number, TOK_DEV // SPAN, N_SEQ, NBR, CAP, 2))(nbr_shard_keys, nbr_shard_turns).reshape((SPANS, NBR))
    nbr_row = touch_ends(jax.random.randint(keys[5], (SPANS, NBR), 0, R_DEV), jax.random.fold_in(keys[5], 1), 0, R_DEV - 1).astype(jnp.int32)
    nbr_count = touch_ends(jax.random.randint(keys[6], (SPANS,), 1, NBR + 1), jax.random.fold_in(keys[6], 1), 1, NBR).astype(jnp.int32)
    return {"hidden": hidden, "query_weight": query_weight, "out_weight": out_weight, "kv_cache": kv_cache, "nbr_shard": nbr_shard, "nbr_row": nbr_row, "nbr_count": nbr_count}


def reference(hidden, query_weight, out_weight, kv_cache, nbr_shard, nbr_row, nbr_count):
    widened = hidden.astype(jnp.float32)
    meansq = lax.optimization_barrier(jnp.mean(widened * widened, axis=1, keepdims=True))
    normed = (widened * lax.rsqrt(meansq + 1e-05)).astype(jnp.bfloat16)
    queries = jnp.dot(normed, query_weight, preferred_element_type=jnp.float32).astype(jnp.bfloat16)
    leading = SPAN - 1
    grouped = jnp.concatenate([queries[leading:], jnp.zeros((leading, D), jnp.bfloat16)], 0)
    grouped = grouped.reshape(SPANS, SPAN, HEADS, HEAD)
    flat_index = (nbr_shard * R_DEV + nbr_row).astype(jnp.int32)

    def one_span(packed):
        group_rows, cache_rows, used_count = packed
        fetched = kv_cache[cache_rows]
        key_rows = fetched[:, 0].reshape(NBR, NBR_LEN, HEADS, HEAD).astype(jnp.float32)
        value_rows = fetched[:, 1].reshape(NBR, NBR_LEN, HEADS, HEAD).astype(jnp.float32)
        scores = jnp.einsum('qhd,nkhd->nhqk', group_rows.astype(jnp.float32), key_rows) * HEAD ** (-0.5)
        highest = lax.optimization_barrier(jnp.max(scores, axis=3))
        expon = jnp.exp(scores - highest[..., None])
        total = lax.optimization_barrier(jnp.sum(expon, axis=3))
        weights = (expon / total[..., None]).astype(jnp.bfloat16)
        part = jnp.einsum('nhqk,nkhd->nqhd', weights.astype(jnp.float32), value_rows).astype(jnp.bfloat16)
        used = (jnp.arange(NBR) < jnp.maximum(used_count, 1))[:, None, None]
        top = lax.optimization_barrier(jnp.max(jnp.where(used, highest, -1e+30), axis=0, keepdims=True))
        safe = jnp.where(used, highest, top)
        scale = jnp.where(used, total * jnp.exp(safe - top), 0.0)
        coef = scale / lax.optimization_barrier(jnp.sum(scale, axis=0, keepdims=True))
        coef_rows = jnp.transpose(coef, (0, 2, 1))[..., None]
        mixed = lax.optimization_barrier(jnp.sum(coef_rows * part.astype(jnp.float32), axis=0))
        return mixed.reshape(SPAN, D).astype(jnp.bfloat16)
    context = lax.map(one_span, (grouped, flat_index, nbr_count)).reshape(SPANS * SPAN, D)
    context = jnp.concatenate([jnp.zeros((leading, D), jnp.bfloat16), context[:TOKENS - leading]], 0)
    column_width = D // N_TP
    summed = jnp.zeros((TOKENS, D), jnp.float32)
    for group_index in range(N_TP):
        lower = group_index * column_width
        upper = lower + column_width
        partial_term = jnp.dot(context[:, lower:upper], out_weight[lower:upper], preferred_element_type=jnp.float32)
        rounded = lax.optimization_barrier(partial_term.astype(jnp.bfloat16))
        summed = summed + rounded.astype(jnp.float32)
    return summed.astype(jnp.bfloat16)
```

```python
import functools

import jax
import jax.numpy as jnp
from jax import lax
from jax.experimental import pallas as pl
from jax.experimental.pallas import tpu as pltpu
from jax.sharding import PartitionSpec as P

F32 = jnp.float32
BF16 = jnp.bfloat16
HEAD = 128
SPAN = 64
SIDE = 4
CAP = 4
HEADS = 4
GROUPS = 16
WIDTH = HEADS * HEAD
OFFSET = (0, -1, 1, 2)
FAR = -1e30
SCORE = 1.4426950408889634 * HEAD**-0.5


def kernel(
    hidden,
    wq,
    wo,
    kv,
    table,
    out,
    hid_v,
    wq_v,
    w2,
    kv_0,
    kv_1,
    kv_2,
    kv_3,
    q_0,
    q_1,
    q_2,
    q_3,
    parts,
    lses,
    tab_v,
    tab_s,
    borrowed,
    sent,
    stats,
    opp,
    opp_stats,
    back,
    back_stats,
    ctx,
    carried,
    far_part,
    far_got,
    near_part,
    near_got,
    own_part,
    swap,
    hid_sem,
    load_sem,
    tab_sem,
    kv_sem,
    q_sem,
    t_sem,
    b_sem,
    w_sem,
    r_sem,
    x_sem,
    z_sem,
    s_sem,
):
    kvbuf = (kv_0, kv_1, kv_2, kv_3)
    qbuf = (q_0, q_1, q_2, q_3)
    seq = lax.axis_index("seq")
    tp = lax.axis_index("tp")
    core = tp % 2
    z = tp // 2
    row, col = seq // SIDE, seq % SIDE
    a = row + core * (col - row)
    b = col + core * (row - col)
    a_step, b_step = SIDE - 3 * core, 1 + 3 * core

    def along_a(by):
        return (lax.rem(a + by + SIDE, SIDE) * a_step + b * b_step, tp)

    def along_b(by):
        return (a * a_step + lax.rem(b + by + SIDE, SIDE) * b_step, tp)

    def along_z(by):
        return (seq, lax.rem(z + by + SIDE, SIDE) * 2 + core)

    sibling = (seq, z * 2 + 1 - core)
    next_block = (lax.rem(seq + 1, 16), tp)
    last_block = (lax.rem(seq + 15, 16), tp)

    def remote(src, dst, sems, at, device):
        return pltpu.make_async_remote_copy(
            src_ref=src,
            dst_ref=dst,
            send_sem=sems.at[0, at],
            recv_sem=sems.at[1, at],
            device_id=device,
            device_id_type=pl.DeviceIdType.MESH,
        )

    started = []

    def send(copy):
        copy.start()
        started.append(copy)

    loads = [pltpu.make_async_copy(wq, wq_v, load_sem.at[0])]
    loads[0].start()
    hid_loads = [
        pltpu.make_async_copy(hidden.at[pl.ds(256 * c, 256), :], hid_v.at[c], hid_sem.at[c])
        for c in range(4)
    ]
    for copy in hid_loads:
        copy.start()
    kv_load = pltpu.make_async_copy(kv, kvbuf[0], load_sem.at[1])
    kv_load.start()
    tab_load = pltpu.make_async_copy(table, tab_s.at[0], tab_sem.at[0])
    tab_load.start()
    w_load = pltpu.make_async_copy(
        wo.at[:, pl.ds(pl.multiple_of(core * 2048, 2048), 2048)], w2.at[core], load_sem.at[2]
    )
    w_load.start()

    barrier = pltpu.get_barrier_semaphore()
    friends = (
        along_a(1), along_a(-1), along_b(1), along_b(-1), along_z(1), along_z(-1),
        sibling, next_block, last_block,
    )
    for device in friends:
        pl.semaphore_signal(barrier, inc=1, device_id=device, device_id_type=pl.DeviceIdType.MESH)
    pl.semaphore_wait(barrier, len(friends))

    low, high = pl.ds(0, 4), pl.ds(4, 4)
    kv_copies = [
        remote(kv.at[low], kvbuf[1].at[low], kv_sem, 0, along_a(1)),
        remote(kv.at[high], kvbuf[2].at[high], kv_sem, 1, along_a(-1)),
        remote(kv.at[high], kvbuf[1].at[high], kv_sem, 2, along_a(1)),
        remote(kv.at[low], kvbuf[2].at[low], kv_sem, 3, along_a(-1)),
        remote(kvbuf[1].at[low], kvbuf[3].at[low], kv_sem, 4, along_a(1)),
        remote(kvbuf[2].at[high], kvbuf[3].at[high], kv_sem, 5, along_a(-1)),
    ]
    for copy in kv_copies[:4]:
        send(copy)
    tab_copies = [
        remote(table, tab_v.at[0], t_sem, 0, along_b(1)),
        remote(table, tab_v.at[1], t_sem, 1, along_b(-1)),
        remote(tab_v.at[0], tab_v.at[2], t_sem, 2, along_b(1)),
    ]
    for copy in tab_copies[:2]:
        send(copy)
    w_copy = remote(
        wo.at[:, pl.ds(pl.multiple_of((1 - core) * 2048, 2048), 2048)], w2.at[core], w_sem, 0, sibling
    )

    lo_g, hi_g = pl.ds(0, 8), pl.ds(8, 8)
    q_copies = [
        remote(qbuf[0].at[lo_g], qbuf[1].at[lo_g], q_sem, 0, along_b(1)),
        remote(qbuf[0].at[hi_g], qbuf[2].at[hi_g], q_sem, 1, along_b(-1)),
        remote(qbuf[0].at[hi_g], qbuf[1].at[hi_g], q_sem, 2, along_b(1)),
        remote(qbuf[0].at[lo_g], qbuf[2].at[lo_g], q_sem, 3, along_b(-1)),
        remote(qbuf[1].at[lo_g], qbuf[3].at[lo_g], q_sem, 4, along_b(1)),
        remote(qbuf[2].at[hi_g], qbuf[3].at[hi_g], q_sem, 5, along_b(-1)),
    ]
    lend = remote(borrowed.at[0], borrowed.at[1], b_sem, 0, last_block)
    loads[0].wait()
    tail = jnp.zeros((1, WIDTH), F32)
    first_row = lax.broadcasted_iota(jnp.int32, (256, WIDTH), 0) == 0
    for c in range(4):
        hid_loads[c].wait()
        square = jnp.zeros((256, HEAD), F32)
        for j in range(32):
            piece = hid_v[c, :, j * HEAD : (j + 1) * HEAD].astype(F32)
            square = square + piece * piece
        scale = lax.rsqrt(jnp.sum(square, axis=1, keepdims=True) * (1.0 / 4096) + 1e-05)
        cols = [
            jnp.dot(hid_v[c], wq_v[:, n * 256 : (n + 1) * 256], preferred_element_type=F32) * scale
            for n in range(2)
        ]
        queries = jnp.concatenate(cols, axis=1)
        moved = jnp.where(first_row, tail, pltpu.roll(queries, 1, 0))
        tail = queries[255:256]
        moved = moved.astype(BF16).reshape(4, SPAN, WIDTH)
        if c == 0:
            borrowed[0] = moved[0]
            send(lend)
            qbuf[0][0:3] = moved[1:4]
        else:
            qbuf[0][4 * c - 1 : 4 * c + 3] = moved
        if c == 2:
            send(q_copies[0])
            send(q_copies[3])
    lend.wait_recv()
    span_row = lax.broadcasted_iota(jnp.int32, (SPAN, WIDTH), 0)
    qbuf[0][15] = jnp.where(span_row == 0, tail, borrowed[1].astype(F32)).astype(BF16)
    send(q_copies[1])
    send(q_copies[2])
    send(w_copy)

    tab_copies[0].wait_recv()
    send(tab_copies[2])
    tab_copies[1].wait_recv()
    tab_copies[2].wait_recv()
    tab_loads = [
        pltpu.make_async_copy(tab_v.at[d], tab_s.at[d + 1], tab_sem.at[d + 1]) for d in range(3)
    ]
    for copy in tab_loads:
        copy.start()
    for copy in [tab_load, *tab_loads]:
        copy.wait()
    kv_load.wait()

    lane = lax.broadcasted_iota(jnp.int32, (SPAN, HEAD), 1)

    def slots(d, i):
        base = lax.rem(a + OFFSET[i] + SIDE, SIDE) * CAP

        def one(k, carry):
            at = base + k
            group = tab_s[d, b, at]
            cached = tab_s[d, b, 16 + at]
            lse = jnp.zeros((SPAN, HEAD), F32)
            for h in range(HEADS):
                cut = slice(h * HEAD, (h + 1) * HEAD)
                query = qbuf[d][group, :, cut]
                keys = kvbuf[i][cached, 0, :, cut]
                values = kvbuf[i][cached, 1, :, cut]
                scores = lax.dot_general(
                    query, keys, (((1,), (1,)), ((), ())), preferred_element_type=F32
                )
                scores = scores * SCORE
                highest = jnp.max(scores, axis=1, keepdims=True)
                expon = jnp.exp2(scores - highest)
                total = jnp.sum(expon, axis=1, keepdims=True)
                part = jnp.dot(expon.astype(BF16), values, preferred_element_type=F32)
                parts[d, at, :, cut] = (part / total).astype(BF16)
                lse = jnp.where(lane == h, highest + jnp.log2(total), lse)
            lses[d, at] = lse
            return carry

        lax.fori_loop(0, CAP, one, 0)

    def merged(sources):
        top = functools.reduce(jnp.maximum, [lse for lse, _ in sources])
        shares = [jnp.exp2(lse - top) for lse, _ in sources]
        whole = functools.reduce(jnp.add, shares)
        inverse = 1.0 / whole
        coefs = [share * inverse for share in shares]
        heads = []
        for h in range(HEADS):
            cut = slice(h * HEAD, (h + 1) * HEAD)
            heads.append(
                functools.reduce(
                    jnp.add,
                    [
                        coef[:, h : h + 1] * part[:, cut].astype(F32)
                        for coef, (_, part) in zip(coefs, sources)
                    ],
                )
            )
        return jnp.concatenate(heads, axis=1), top + jnp.log2(whole)

    def from_slots(d, g):
        found = []
        for n in range(2):
            at = tab_s[d, b, 32 + 2 * g + n]
            used = tab_s[d, b, 64 + 2 * g + n]
            lse = jnp.where(jnp.full((SPAN, HEAD), used, jnp.int32) > 0, lses[d, at], FAR)
            found.append((lse, parts[d, at]))
        return found

    def stats_of(held, g):
        return pltpu.roll(held, lax.rem(HEAD - HEADS * g, HEAD), 1)

    def contribute(d, first, last, extra, held):
        def one(g, held):
            sources = from_slots(d, g)
            if extra is not None:
                sources.append((stats_of(opp_stats[extra], g), opp[extra, g - first]))
            mixed, lse = merged(sources)
            sent[d - 1, g] = mixed.astype(BF16)
            return jnp.where(lane // HEADS == g, pltpu.roll(lse, HEADS * g, 1), held)

        return lax.fori_loop(first, last, one, held)

    kv_copies[0].wait_recv()
    send(kv_copies[4])
    kv_copies[1].wait_recv()
    send(kv_copies[5])
    q_copies[0].wait_recv()
    send(q_copies[4])
    q_copies[1].wait_recv()
    send(q_copies[5])
    slots(0, 0)
    q_copies[2].wait_recv()
    q_copies[3].wait_recv()
    slots(1, 0)
    slots(2, 0)
    kv_copies[2].wait_recv()
    kv_copies[3].wait_recv()
    for d in range(3):
        slots(d, 1)
        slots(d, 2)
    q_copies[4].wait_recv()
    q_copies[5].wait_recv()
    for i in range(3):
        slots(3, i)
    kv_copies[4].wait_recv()
    kv_copies[5].wait_recv()

    none = jnp.zeros((SPAN, HEAD), F32)
    opp_copies = [
        remote(sent.at[2, lo_g], opp.at[0], r_sem, 0, along_b(1)),
        remote(stats.at[2], opp_stats.at[0], r_sem, 1, along_b(1)),
        remote(sent.at[2, hi_g], opp.at[1], r_sem, 2, along_b(-1)),
        remote(stats.at[2], opp_stats.at[1], r_sem, 3, along_b(-1)),
    ]
    back_copies = [
        remote(sent.at[1, hi_g], back.at[0, hi_g], r_sem, 4, along_b(1)),
        remote(sent.at[1, lo_g], back.at[0, lo_g], r_sem, 5, along_b(1)),
        remote(stats.at[1], back_stats.at[0], r_sem, 6, along_b(1)),
        remote(sent.at[0, lo_g], back.at[1, lo_g], r_sem, 7, along_b(-1)),
        remote(sent.at[0, hi_g], back.at[1, hi_g], r_sem, 8, along_b(-1)),
        remote(stats.at[0], back_stats.at[1], r_sem, 9, along_b(-1)),
    ]
    slots(3, 3)
    stats[2] = contribute(3, 0, GROUPS, None, none)
    for copy in opp_copies:
        send(copy)
    slots(2, 3)
    held_next = contribute(2, 8, GROUPS, None, none)
    send(back_copies[0])
    slots(1, 3)
    held_last = contribute(1, 0, 8, None, none)
    send(back_copies[3])
    slots(0, 3)
    opp_copies[0].wait_recv()
    opp_copies[1].wait_recv()
    stats[1] = contribute(2, 0, 8, 0, held_next)
    send(back_copies[1])
    send(back_copies[2])
    opp_copies[2].wait_recv()
    opp_copies[3].wait_recv()
    stats[0] = contribute(1, 8, GROUPS, 1, held_last)
    send(back_copies[4])
    send(back_copies[5])
    for copy in back_copies:
        copy.wait_recv()

    carry_copy = remote(carried.at[0], carried.at[1], b_sem, 1, next_block)

    def finish(g):
        sources = from_slots(0, g)
        sources.append((stats_of(back_stats[0], g), back[0, g]))
        sources.append((stats_of(back_stats[1], g), back[1, g]))
        return merged(sources)[0]

    mixed = finish(GROUPS - 1)
    carried[0] = pltpu.roll(mixed, SPAN - 1, 0).astype(BF16)
    send(carry_copy)

    def one_span(step, head_row):
        g = GROUPS - 2 - step
        mixed = finish(g)
        moved = jnp.where(span_row == SPAN - 1, head_row, pltpu.roll(mixed, SPAN - 1, 0))
        ctx[core, g + 1] = moved.astype(BF16)
        return mixed[0:1]

    head_row = lax.fori_loop(0, GROUPS - 1, one_span, mixed[0:1])
    carry_copy.wait_recv()
    arrived = jnp.where(jnp.full((SPAN, WIDTH), seq, jnp.int32) > 0, carried[1].astype(F32), 0.0)
    ctx[core, 0] = jnp.where(span_row == SPAN - 1, head_row, arrived).astype(BF16)

    ctx_copy = remote(ctx.at[core], ctx.at[core], x_sem, 0, sibling)
    send(ctx_copy)
    w_load.wait()
    w_copy.wait_recv()
    ctx_copy.wait_recv()

    def project(by, half, write):
        start = lax.rem(z + by + SIDE, SIDE) * 4
        left = ctx[0, pl.ds(start, 4)].reshape(256, WIDTH)
        right = ctx[1, pl.ds(start, 4)].reshape(256, WIDTH)

        def one(n, carry):
            at = pl.ds(pl.multiple_of(half * 1024 + n * 256, 256), 256)
            total = jnp.dot(left, w2[0, :, at], preferred_element_type=F32)
            total = total + jnp.dot(right, w2[1, :, at], preferred_element_type=F32)
            write(pl.ds(pl.multiple_of(n * 256, 256), 256), total)
            return carry

        lax.fori_loop(0, 4, one, 0)

    far_copies = [
        remote(far_part.at[0], far_got.at[0], z_sem, 0, along_z(1)),
        remote(far_part.at[1], far_got.at[1], z_sem, 1, along_z(-1)),
    ]
    near_copies = [
        [remote(near_part.at[0, h], near_got.at[0, h], z_sem, 2 + h, along_z(1)) for h in range(2)],
        [remote(near_part.at[1, h], near_got.at[1, h], z_sem, 4 + h, along_z(-1)) for h in range(2)],
    ]

    for half in range(2):

        def write_far(at, total, half=half):
            far_part[half, :, at] = total.astype(BF16)

        project(2, half, write_far)
        send(far_copies[half])

    def near(way, half, got):
        def write_near(at, total):
            if got is not None:
                total = total + far_got[got, :, at].astype(F32)
            near_part[way, half, :, at] = total.astype(BF16)

        project(1 - 2 * way, half, write_near)
        send(near_copies[way][half])

    near(0, 1, None)
    near(1, 0, None)
    far_copies[0].wait_recv()
    near(0, 0, 0)
    far_copies[1].wait_recv()
    near(1, 1, 1)

    mine = pl.ds(pl.multiple_of(core * 128, 128), 128)
    theirs = pl.ds(pl.multiple_of((1 - core) * 128, 128), 128)
    swap_copies = [
        remote(own_part.at[half, theirs], swap.at[half], s_sem, half, sibling) for half in range(2)
    ]
    for half in (1, 0):
        near_copies[0][half].wait_recv()
        near_copies[1][half].wait_recv()

        def write_own(at, total, half=half):
            total = total + near_got[0, half, :, at].astype(F32)
            total = total + near_got[1, half, :, at].astype(F32)
            own_part[half, :, at] = total.astype(BF16)

        project(0, half, write_own)
        send(swap_copies[half])
        out[:, pl.ds(pl.multiple_of(core * 2048 + half * 1024, 1024), 1024)] = own_part[half, mine]
    for half in (1, 0):
        swap_copies[half].wait_recv()
        out[:, pl.ds(pl.multiple_of((1 - core) * 2048 + half * 1024, 1024), 1024)] = swap[half]
    for copy in started:
        copy.wait_send()


def tables(nbr_shard, nbr_row, nbr_count):
    core = lax.axis_index("tp") % 2
    owners = nbr_shard.reshape(-1)
    wanted = nbr_row.reshape(-1)
    pairs = owners.shape[0]
    at = jnp.arange(pairs)
    before = (owners[:, None] == owners[None, :]) & (at[None, :] < at[:, None])
    rank = jnp.sum(before.astype(jnp.int32), axis=1)
    used = (at % 2) < jnp.maximum(nbr_count, 1)[at // 2]
    owner_a = jnp.where(core == 0, owners // SIDE, owners % SIDE)
    owner_b = jnp.where(core == 0, owners % SIDE, owners // SIDE)
    slot = owner_a * CAP + rank
    ring = jnp.arange(8)[:, None]
    here = owner_b[None, :] == ring
    match = here[:, None, :] & (slot[None, None, :] == jnp.arange(16)[None, :, None])
    group_at = jnp.sum(jnp.where(match, (at // 2)[None, None, :], 0), axis=2)
    row_at = jnp.sum(jnp.where(match, wanted[None, None, :], 0), axis=2)
    slot_at = jnp.where(here, slot[None, :], 0)
    used_at = (here & used[None, :]).astype(jnp.int32)
    filler = jnp.zeros((8, 32), jnp.int32)
    return jnp.concatenate([group_at, row_at, slot_at, used_at, filler], axis=1).astype(jnp.int32)


def shards(hidden, query_weight, out_weight, kv_cache, nbr_shard, nbr_row, nbr_count):
    table = tables(nbr_shard, nbr_row, nbr_count)
    dma = pltpu.SemaphoreType.DMA
    hbm = pl.BlockSpec(memory_space=pl.ANY)
    return pl.pallas_call(
        kernel,
        out_shape=jax.ShapeDtypeStruct((128, 4096), BF16),
        in_specs=[hbm] * 5,
        out_specs=pl.BlockSpec(memory_space=pltpu.VMEM),
        scratch_shapes=[
            pltpu.VMEM((4, 256, 4096), BF16),
            pltpu.VMEM((4096, WIDTH), BF16),
            pltpu.VMEM((2, WIDTH, 2048), BF16),
            *[pltpu.VMEM((8, 2, 128, WIDTH), BF16)] * 4,
            *[pltpu.VMEM((GROUPS, SPAN, WIDTH), BF16)] * 4,
            pltpu.VMEM((4, 16, SPAN, WIDTH), BF16),
            pltpu.VMEM((4, 16, SPAN, HEAD), F32),
            pltpu.VMEM((3, 8, 128), jnp.int32),
            pltpu.SMEM((4, 8, 128), jnp.int32),
            pltpu.VMEM((2, SPAN, WIDTH), BF16),
            pltpu.VMEM((3, GROUPS, SPAN, WIDTH), BF16),
            pltpu.VMEM((3, SPAN, HEAD), F32),
            pltpu.VMEM((2, 8, SPAN, WIDTH), BF16),
            pltpu.VMEM((2, SPAN, HEAD), F32),
            pltpu.VMEM((2, GROUPS, SPAN, WIDTH), BF16),
            pltpu.VMEM((2, SPAN, HEAD), F32),
            pltpu.VMEM((2, GROUPS, SPAN, WIDTH), BF16),
            pltpu.VMEM((2, SPAN, WIDTH), BF16),
            pltpu.VMEM((2, 256, 1024), BF16),
            pltpu.VMEM((2, 256, 1024), BF16),
            pltpu.VMEM((2, 2, 256, 1024), BF16),
            pltpu.VMEM((2, 2, 256, 1024), BF16),
            pltpu.VMEM((2, 256, 1024), BF16),
            pltpu.VMEM((2, 128, 1024), BF16),
            dma((4,)),
            dma((3,)),
            dma((4,)),
            dma((2, 6)),
            dma((2, 6)),
            dma((2, 3)),
            dma((2, 2)),
            dma((2, 1)),
            dma((2, 10)),
            dma((2, 1)),
            dma((2, 6)),
            dma((2, 2)),
        ],
        compiler_params=pltpu.CompilerParams(
            collective_id=0, has_side_effects=True, vmem_limit_bytes=62 * 1024 * 1024
        ),
        cost_estimate=pl.CostEstimate(flops=9_000_000_000, bytes_accessed=20_000_000, transcendentals=2_000_000),
    )(hidden, query_weight, out_weight, kv_cache, table)


def solution(mesh):
    placed = (
        P("seq", None),
        P(None, "tp"),
        P("tp", None),
        P("seq", None, None, "tp"),
        P("seq", None),
        P("seq", None),
        P("seq"),
    )
    return jax.shard_map(
        shards, mesh=mesh, in_specs=placed, out_specs=P(("seq", "tp"), None), check_vma=False
    )
```

```python
import functools

import jax
import jax.numpy as jnp
from jax import lax
from jax.experimental import pallas as pl
from jax.experimental.pallas import tpu as pltpu
from jax.sharding import PartitionSpec as P

F32 = jnp.float32
BF16 = jnp.bfloat16
HEAD = 128
SPAN = 64
SIDE = 4
CAP = 4
HEADS = 4
GROUPS = 16
WIDTH = HEADS * HEAD
OFFSET = (0, -1, 1, 2)
FAR = -1e30
SCORE = 1.4426950408889634 * HEAD**-0.5


def slot_table(core, shard_of, row_of, count_of):
    ring = lax.broadcasted_iota(jnp.int32, (8, 128), 0)
    lane = lax.broadcasted_iota(jnp.int32, (8, 128), 1)
    table = jnp.zeros((8, 128), jnp.int32)
    pairs = 2 * GROUPS
    owners = [shard_of[e % 2, e // 2] for e in range(pairs)]
    for e, owner in enumerate(owners):
        rank = jnp.int32(0)
        for other in owners[:e]:
            rank = rank + jnp.where(other == owner, 1, 0)
        down, across = owner // SIDE, owner % SIDE
        owner_a = down + core * (across - down)
        owner_b = across + core * (down - across)
        slot = owner_a * CAP + jnp.minimum(rank, CAP - 1)
        fits = jnp.where(rank < CAP, 0, 96)
        entry = jnp.where(lane == slot + fits, e // 2, 0)
        entry = entry + jnp.where(lane == 16 + slot + fits, row_of[e % 2, e // 2], 0)
        entry = entry + jnp.where(lane == 32 + e, slot, 0)
        if e % 2 == 0:
            used = jnp.int32(1)
        else:
            used = jnp.where(count_of[e // 2] > 1, 1, 0)
        entry = entry + jnp.where(lane == 64 + e, used, 0)
        table = table + jnp.where(ring == owner_b, entry, 0)
    return table


def kernel(
    hidden, wq, wo, kv, shard_of, row_of, count_of, out,
    hid_v, wq_v, w_all, kvs, qs, parts, lses, table, tab_v, tab_s, borrowed, sent, stats, opp, opp_stats,
    back, back_stats, ctx, carried, total, keep, give, got, ship, landed,
    hid_sem, load_sem, tab_sem, kv_sem, q_sem, t_sem, b_sem, c_sem, w_sem, r_sem, x_sem, g_sem, s_sem,
):
    seq = lax.axis_index("seq")
    tp = lax.axis_index("tp")
    core = tp % 2
    z = tp // 2
    row, col = seq // SIDE, seq % SIDE
    a = row + core * (col - row)
    b = col + core * (row - col)
    a_step, b_step = SIDE - 3 * core, 1 + 3 * core

    def along_a(by):
        return (lax.rem(a + by + SIDE, SIDE) * a_step + b * b_step, tp)

    def along_b(by):
        return (a * a_step + lax.rem(b + by + SIDE, SIDE) * b_step, tp)

    def along_z(by):
        return (seq, lax.rem(z + by + SIDE, SIDE) * 2 + core)

    sibling = (seq, z * 2 + 1 - core)
    next_block = (lax.rem(seq + 1, 16), tp)
    last_block = (lax.rem(seq + 15, 16), tp)

    def remote(src, dst, sems, at, device):
        return pltpu.make_async_remote_copy(
            src_ref=src,
            dst_ref=dst,
            send_sem=sems.at[(0, *at)],
            recv_sem=sems.at[(1, *at)],
            device_id=device,
            device_id_type=pl.DeviceIdType.MESH,
        )

    started = []

    def send(copy):
        copy.start()
        started.append(copy)

    def arrive(*copies):
        for copy in copies:
            copy.wait_recv()

    wq_load = pltpu.make_async_copy(wq, wq_v, load_sem.at[0])
    wq_load.start()
    hid_loads = [
        pltpu.make_async_copy(hidden.at[pl.ds(256 * c, 256), :], hid_v.at[c], hid_sem.at[c])
        for c in range(4)
    ]
    for copy in hid_loads:
        copy.start()
    lanes = [pl.ds(h * HEAD, HEAD) for h in range(HEADS)]
    kv_loads = [
        pltpu.make_async_copy(kv.at[:, :, :, lanes[h]], kvs[0][h], load_sem.at[1 + h])
        for h in range(HEADS)
    ]
    for copy in kv_loads:
        copy.start()

    def columns(of):
        return pl.ds(pl.multiple_of(of * 1024, 1024), 1024)

    w_load = pltpu.make_async_copy(wo.at[:, columns(z)], w_all.at[z], load_sem.at[5])
    w_load.start()

    barrier = pltpu.get_barrier_semaphore()
    friends = (
        along_a(1), along_a(-1), along_b(1), along_b(-1), along_z(1), along_z(-1), along_z(2),
        sibling, next_block, last_block,
    )
    for device in friends:
        pl.semaphore_signal(barrier, inc=1, device_id=device, device_id_type=pl.DeviceIdType.MESH)
    pl.semaphore_wait(barrier, len(friends))

    low, high = pl.ds(0, 4), pl.ds(4, 4)
    kv_copies = [
        [
            remote(kv.at[low, :, :, lanes[h]], kvs[1][h].at[low], kv_sem, (h, 0), along_a(1)),
            remote(kv.at[high, :, :, lanes[h]], kvs[2][h].at[high], kv_sem, (h, 1), along_a(-1)),
            remote(kv.at[high, :, :, lanes[h]], kvs[1][h].at[high], kv_sem, (h, 2), along_a(1)),
            remote(kv.at[low, :, :, lanes[h]], kvs[2][h].at[low], kv_sem, (h, 3), along_a(-1)),
            remote(kvs[1][h].at[low], kvs[3][h].at[low], kv_sem, (h, 4), along_a(1)),
            remote(kvs[2][h].at[high], kvs[3][h].at[high], kv_sem, (h, 5), along_a(-1)),
        ]
        for h in range(HEADS)
    ]
    tab_copies = [
        remote(table, tab_v.at[0], t_sem, (0,), along_b(1)),
        remote(table, tab_v.at[1], t_sem, (1,), along_b(-1)),
        remote(tab_v.at[0], tab_v.at[2], t_sem, (2,), along_b(1)),
    ]
    w_copies = [
        remote(wo.at[:, columns(lax.rem(z + by + SIDE, SIDE))], w_all.at[z], w_sem, (j,), along_z(by))
        for j, by in enumerate((1, -1, 2))
    ]
    for h in range(2):
        for copy in kv_copies[h][:4]:
            send(copy)
    table[...] = slot_table(core, shard_of, row_of, count_of)
    for copy in tab_copies[:2]:
        send(copy)
    tab_load = pltpu.make_async_copy(table, tab_s.at[0], tab_sem.at[0])
    tab_load.start()
    for copy in w_copies:
        send(copy)

    lo_g, hi_g = pl.ds(0, 8), pl.ds(8, 8)
    q_copies = [
        [
            remote(qs[0][h].at[lo_g], qs[1][h].at[lo_g], q_sem, (h, 0), along_b(1)),
            remote(qs[0][h].at[hi_g], qs[2][h].at[hi_g], q_sem, (h, 1), along_b(-1)),
            remote(qs[0][h].at[hi_g], qs[1][h].at[hi_g], q_sem, (h, 2), along_b(1)),
            remote(qs[0][h].at[lo_g], qs[2][h].at[lo_g], q_sem, (h, 3), along_b(-1)),
            remote(qs[1][h].at[lo_g], qs[3][h].at[lo_g], q_sem, (h, 4), along_b(1)),
            remote(qs[2][h].at[hi_g], qs[3][h].at[hi_g], q_sem, (h, 5), along_b(-1)),
        ]
        for h in range(HEADS)
    ]
    lend = remote(borrowed.at[0], borrowed.at[1], b_sem, (), last_block)
    wq_load.wait()
    tail = jnp.zeros((1, WIDTH), F32)
    first_row = lax.broadcasted_iota(jnp.int32, (256, WIDTH), 0) == 0
    for c in range(4):
        hid_loads[c].wait()
        square = jnp.zeros((256, HEAD), F32)
        for j in range(32):
            piece = hid_v[c, :, j * HEAD : (j + 1) * HEAD].astype(F32)
            square = square + piece * piece
        scale = lax.rsqrt(jnp.sum(square, axis=1, keepdims=True) * (1.0 / 4096) + 1e-05)
        cols = [
            jnp.dot(hid_v[c], wq_v[:, n * 256 : (n + 1) * 256], preferred_element_type=F32) * scale
            for n in range(2)
        ]
        queries = jnp.concatenate(cols, axis=1)
        moved = jnp.where(first_row, tail, pltpu.roll(queries, 1, 0))
        tail = queries[255:256]
        moved = moved.astype(BF16).reshape(4, SPAN, WIDTH)
        if c == 0:
            borrowed[0] = moved[0]
            send(lend)
        for h in range(HEADS):
            cut = slice(h * HEAD, (h + 1) * HEAD)
            if c == 0:
                qs[0][h][0:3] = moved[1:4, :, cut]
            else:
                qs[0][h][4 * c - 1 : 4 * c + 3] = moved[:, :, cut]
        if c == 2:
            send(q_copies[0][0])
            send(q_copies[0][3])
    arrive(lend)
    span_row = lax.broadcasted_iota(jnp.int32, (SPAN, HEAD), 0)
    for h in range(HEADS):
        cut = slice(h * HEAD, (h + 1) * HEAD)
        last = jnp.where(span_row == 0, tail[:, cut], borrowed[1, :, cut].astype(F32))
        qs[0][h][15] = last.astype(BF16)
    send(q_copies[0][1])
    send(q_copies[0][2])
    for copy in q_copies[1][:4]:
        send(copy)

    arrive(tab_copies[0])
    send(tab_copies[2])
    arrive(tab_copies[1], tab_copies[2])
    tab_loads = [
        pltpu.make_async_copy(tab_v.at[d], tab_s.at[d + 1], tab_sem.at[d + 1]) for d in range(3)
    ]
    for copy in tab_loads:
        copy.start()
    for copy in [tab_load, *tab_loads, *kv_loads]:
        copy.wait()

    lane = lax.broadcasted_iota(jnp.int32, (SPAN, HEAD), 1)

    def slots(h, d, i):
        base = lax.rem(a + OFFSET[i] + SIDE, SIDE) * CAP
        spots = [base + k for k in range(CAP)]
        values, scores = [], []
        for at in spots:
            query = qs[d][h][tab_s[d, b, at]]
            cached = tab_s[d, b, 16 + at]
            values.append(kvs[i][h][cached, 1])
            scores.append(
                lax.dot_general(
                    query,
                    kvs[i][h][cached, 0],
                    (((1,), (1,)), ((), ())),
                    preferred_element_type=F32,
                )
                * SCORE
            )
        highest = [jnp.max(score, axis=1, keepdims=True) for score in scores]
        expon = [jnp.exp2(score - high) for score, high in zip(scores, highest)]
        totals = [jnp.sum(one, axis=1, keepdims=True) for one in expon]
        for at, one, value, high, whole in zip(spots, expon, values, highest, totals):
            part = jnp.dot(one.astype(BF16), value, preferred_element_type=F32)
            parts[h % 2, d, at] = part * (1.0 / whole)
            lses[h % 2, d, at] = jnp.broadcast_to(high + jnp.log2(whole), (SPAN, HEAD))

    def merged(sources):
        top = functools.reduce(jnp.maximum, [lse for lse, _ in sources])
        shares = [jnp.exp2(lse - top) for lse, _ in sources]
        whole = functools.reduce(jnp.add, shares)
        mixed = functools.reduce(
            jnp.add, [share * part.astype(F32) for share, (_, part) in zip(shares, sources)]
        )
        return mixed * (1.0 / whole), top + jnp.log2(whole)

    def from_slots(h, d, g):
        found = []
        for n in range(2):
            at = tab_s[d, b, 32 + 2 * g + n]
            used = tab_s[d, b, 64 + 2 * g + n]
            lse = jnp.where(jnp.full((SPAN, HEAD), used, jnp.int32) > 0, lses[h % 2, d, at], FAR)
            found.append((lse, parts[h % 2, d, at]))
        return found

    def stats_of(held, g):
        turned = pltpu.roll(held, lax.rem(HEAD - g, HEAD), 1)
        return jnp.broadcast_to(turned[:, 0:1], (SPAN, HEAD))

    def contribute(h, d, first, last, extra, held):
        def one(g, held):
            sources = from_slots(h, d, g)
            if extra is not None:
                sources.append((stats_of(opp_stats[h, extra], g), opp[h, extra, g - first]))
            mixed, lse = merged(sources)
            sent[h, d - 1, g] = mixed.astype(BF16)
            return jnp.where(lane == g, lse, held)

        return lax.fori_loop(first, last, one, held, unroll=4)

    none = jnp.zeros((SPAN, HEAD), F32)
    opp_copies = [
        [
            remote(sent.at[h, 2, lo_g], opp.at[h, 0], r_sem, (h, 0), along_b(1)),
            remote(stats.at[h, 2], opp_stats.at[h, 0], r_sem, (h, 1), along_b(1)),
            remote(sent.at[h, 2, hi_g], opp.at[h, 1], r_sem, (h, 2), along_b(-1)),
            remote(stats.at[h, 2], opp_stats.at[h, 1], r_sem, (h, 3), along_b(-1)),
        ]
        for h in range(HEADS)
    ]
    back_copies = [
        [
            remote(sent.at[h, 1, hi_g], back.at[h, 0, hi_g], r_sem, (h, 4), along_b(1)),
            remote(sent.at[h, 1, lo_g], back.at[h, 0, lo_g], r_sem, (h, 5), along_b(1)),
            remote(stats.at[h, 1], back_stats.at[h, 0], r_sem, (h, 6), along_b(1)),
            remote(sent.at[h, 0, lo_g], back.at[h, 1, lo_g], r_sem, (h, 7), along_b(-1)),
            remote(sent.at[h, 0, hi_g], back.at[h, 1, hi_g], r_sem, (h, 8), along_b(-1)),
            remote(stats.at[h, 0], back_stats.at[h, 1], r_sem, (h, 9), along_b(-1)),
        ]
        for h in range(HEADS)
    ]
    carry_copies = [
        remote(carried.at[0, h], carried.at[1, h], c_sem, (h,), next_block) for h in range(HEADS)
    ]
    before, after = lax.rem(z + 3, SIDE), lax.rem(z + 1, SIDE)
    ctx_copies = [
        [
            remote(ctx.at[h, z], ctx.at[h, z], x_sem, (h, 0), along_z(1)),
            remote(ctx.at[h, z], ctx.at[h, z], x_sem, (h, 1), along_z(-1)),
            remote(ctx.at[h, before, lo_g], ctx.at[h, before, lo_g], x_sem, (h, 2), along_z(1)),
            remote(ctx.at[h, after, hi_g], ctx.at[h, after, hi_g], x_sem, (h, 3), along_z(-1)),
        ]
        for h in range(HEADS)
    ]

    def pass_on(h):
        arrive(kv_copies[h][0])
        send(kv_copies[h][4])
        arrive(kv_copies[h][1])
        send(kv_copies[h][5])
        arrive(q_copies[h][0])
        send(q_copies[h][4])
        arrive(q_copies[h][1])
        send(q_copies[h][5])
        if h + 2 < HEADS:
            for copy in kv_copies[h + 2][:4] + q_copies[h + 2][:4]:
                send(copy)
        arrive(*kv_copies[h][2:4], *q_copies[h][2:4])

    def finish(h, g):
        sources = from_slots(h, 0, g)
        sources.append((stats_of(back_stats[h, 0], g), back[h, 0, g]))
        sources.append((stats_of(back_stats[h, 1], g), back[h, 1, g]))
        return merged(sources)[0]

    def early(h):
        for d in range(3):
            for i in range(3):
                slots(h, d, i)

    def late(h):
        arrive(*q_copies[h][4:6])
        for i in range(3):
            slots(h, 3, i)
        arrive(*kv_copies[h][4:6])
        slots(h, 3, 3)
        stats[h, 2] = contribute(h, 3, 0, GROUPS, None, none)
        for copy in opp_copies[h]:
            send(copy)
        slots(h, 2, 3)
        held_next = contribute(h, 2, 8, GROUPS, None, none)
        send(back_copies[h][0])
        slots(h, 1, 3)
        held_last = contribute(h, 1, 0, 8, None, none)
        send(back_copies[h][3])
        slots(h, 0, 3)
        return held_next, held_last

    def give_back(h, held_next, held_last):
        arrive(*opp_copies[h][0:2])
        stats[h, 1] = contribute(h, 2, 0, 8, 0, held_next)
        send(back_copies[h][1])
        send(back_copies[h][2])
        arrive(*opp_copies[h][2:4])
        stats[h, 0] = contribute(h, 1, 8, GROUPS, 1, held_last)
        send(back_copies[h][4])
        send(back_copies[h][5])

    head_rows = {}

    def context(h):
        arrive(*back_copies[h])
        mixed = finish(h, GROUPS - 1)
        carried[0, h] = pltpu.roll(mixed, SPAN - 1, 0).astype(BF16)
        send(carry_copies[h])

        def one_span(step, head_row):
            g = GROUPS - 2 - step
            mixed = finish(h, g)
            moved = jnp.where(span_row == SPAN - 1, head_row, pltpu.roll(mixed, SPAN - 1, 0))
            ctx[h, z, g + 1] = moved.astype(BF16)
            return mixed[0:1]

        head_rows[h] = lax.fori_loop(0, GROUPS - 1, one_span, mixed[0:1], unroll=5)

    def context_out(h):
        arrive(carry_copies[h])
        here = jnp.full((SPAN, HEAD), seq, jnp.int32) > 0
        arrived = jnp.where(here, carried[1, h].astype(F32), 0.0)
        ctx[h, z, 0] = jnp.where(span_row == SPAN - 1, head_rows[h], arrived).astype(BF16)
        send(ctx_copies[h][0])
        send(ctx_copies[h][1])

    def context_on(h):
        arrive(ctx_copies[h][0])
        send(ctx_copies[h][2])
        arrive(ctx_copies[h][1])
        send(ctx_copies[h][3])

    def product(h, at, n):
        left = jnp.concatenate([ctx[h, j, at].reshape(-1, HEAD) for j in range(SIDE)], axis=1)
        cut = pl.ds(pl.multiple_of(n * 256, 256), 256)
        right = jnp.concatenate(
            [w_all[j, h * HEAD : (h + 1) * HEAD, cut] for j in range(SIDE)], axis=0
        )
        return jnp.dot(left, right, preferred_element_type=F32), cut

    def project(h):
        if h == 0:
            w_load.wait()
            arrive(*w_copies)
        arrive(*ctx_copies[h][2:4])

        def one(step, carry):
            at = pl.ds((step // 4) * 4, 4)
            value, cut = product(h, at, step % 4)
            value = value.reshape(4, SPAN, 256)
            total[at, :, cut] = value if h == 0 else total[at, :, cut] + value
            return carry

        lax.fori_loop(0, 16, one, 0)

    pass_on(0)
    held = [None] * HEADS
    for h in range(HEADS):
        early(h)
        if h + 1 < HEADS:
            pass_on(h + 1)
        if h >= 1:
            give_back(h - 1, *held[h - 1])
        if h >= 2:
            context_out(h - 2)
        held[h] = late(h)
        if h >= 1:
            context(h - 1)
        if h >= 2:
            context_on(h - 2)
        if h >= 3:
            project(h - 3)
    h = HEADS - 1
    give_back(h, *held[h])
    context_out(h - 1)
    project(h - 2)
    context(h)
    context_on(h - 1)
    context_out(h)
    project(h - 1)
    context_on(h)
    arrive(*ctx_copies[h][2:4])

    ways = (2, 1, -1, 0)
    give_copies = [
        remote(give.at[j], got.at[j], g_sem, (j,), sibling) for j in range(SIDE)
    ]
    ship_copies = [
        remote(ship.at[j], landed.at[j], s_sem, (j,), along_z(by)) for j, by in enumerate(ways[:3])
    ]
    for j, by in enumerate(ways):
        first = lax.rem(z + by + SIDE, SIDE) * 4
        for whose, to in ((1 - core, give), (core, keep)):
            at = pl.ds(first + 2 * whose, 2)

            def one(n, carry, at=at, to=to, j=j):
                value, cut = product(h, at, n)
                value = value + total[at, :, cut].reshape(128, 256)
                to[j, :, cut] = value.astype(to.dtype)
                return carry

            lax.fori_loop(0, 4, one, 0)
            if to is give:
                send(give_copies[j])
    for j, by in enumerate(ways):
        arrive(give_copies[j])
        value = (keep[j] + got[j].astype(F32)).astype(BF16)
        if by == 0:
            out[:, columns(z)] = value
        else:
            ship[j] = value
            send(ship_copies[j])
    for j in (1, 2, 0):
        arrive(ship_copies[j])
        out[:, columns(lax.rem(z - ways[j] + SIDE, SIDE))] = landed[j]
    for copy in started:
        copy.wait_send()


def shards(hidden, query_weight, out_weight, kv_cache, nbr_shard, nbr_row, nbr_count):
    dma = pltpu.SemaphoreType.DMA
    hbm = pl.BlockSpec(memory_space=pl.ANY)
    return pl.pallas_call(
        kernel,
        out_shape=jax.ShapeDtypeStruct((128, 4096), BF16),
        in_specs=[hbm] * 4 + [pl.BlockSpec(memory_space=pltpu.SMEM)] * 3,
        out_specs=pl.BlockSpec(memory_space=pltpu.VMEM),
        scratch_shapes=[
            pltpu.VMEM((4, 256, 4096), BF16),
            pltpu.VMEM((4096, WIDTH), BF16),
            pltpu.VMEM((SIDE, WIDTH, 1024), BF16),
            [[pltpu.VMEM((8, 2, 128, HEAD), BF16)] * HEADS] * SIDE,
            [[pltpu.VMEM((GROUPS, SPAN, HEAD), BF16)] * HEADS] * SIDE,
            pltpu.VMEM((2, SIDE, 16, SPAN, HEAD), F32),
            pltpu.VMEM((2, SIDE, 16, SPAN, HEAD), F32),
            pltpu.VMEM((8, 128), jnp.int32),
            pltpu.VMEM((3, 8, 128), jnp.int32),
            pltpu.SMEM((4, 8, 128), jnp.int32),
            pltpu.VMEM((2, SPAN, WIDTH), BF16),
            pltpu.VMEM((HEADS, 3, GROUPS, SPAN, HEAD), BF16),
            pltpu.VMEM((HEADS, 3, SPAN, HEAD), F32),
            pltpu.VMEM((HEADS, 2, 8, SPAN, HEAD), BF16),
            pltpu.VMEM((HEADS, 2, SPAN, HEAD), F32),
            pltpu.VMEM((HEADS, 2, GROUPS, SPAN, HEAD), BF16),
            pltpu.VMEM((HEADS, 2, SPAN, HEAD), F32),
            pltpu.VMEM((HEADS, SIDE, GROUPS, SPAN, HEAD), BF16),
            pltpu.VMEM((2, HEADS, SPAN, HEAD), BF16),
            pltpu.VMEM((GROUPS, SPAN, 1024), F32),
            pltpu.VMEM((SIDE, 128, 1024), F32),
            pltpu.VMEM((SIDE, 128, 1024), BF16),
            pltpu.VMEM((SIDE, 128, 1024), BF16),
            pltpu.VMEM((3, 128, 1024), BF16),
            pltpu.VMEM((3, 128, 1024), BF16),
            dma((4,)),
            dma((6,)),
            dma((4,)),
            dma((2, HEADS, 6)),
            dma((2, HEADS, 6)),
            dma((2, 3)),
            dma((2,)),
            dma((2, HEADS)),
            dma((2, 3)),
            dma((2, HEADS, 10)),
            dma((2, HEADS, 4)),
            dma((2, SIDE)),
            dma((2, 3)),
        ],
        compiler_params=pltpu.CompilerParams(
            collective_id=0, has_side_effects=True, vmem_limit_bytes=62 * 1024 * 1024
        ),
        cost_estimate=pl.CostEstimate(flops=9_000_000_000, bytes_accessed=20_000_000, transcendentals=2_000_000),
    )(hidden, query_weight, out_weight, kv_cache, nbr_shard.T, nbr_row.T, nbr_count)


def solution(mesh):
    placed = (
        P("seq", None),
        P(None, "tp"),
        P("tp", None),
        P("seq", None, None, "tp"),
        P("seq", None),
        P("seq", None),
        P("seq"),
    )
    return jax.shard_map(
        shards, mesh=mesh, in_specs=placed, out_specs=P(("seq", "tp"), None), check_vma=False
    )
```

```python
import functools

import jax
import jax.numpy as jnp
from jax import lax
from jax.experimental import pallas as pl
from jax.experimental.pallas import tpu as pltpu
from jax.sharding import PartitionSpec as P

F32 = jnp.float32
BF16 = jnp.bfloat16
HEAD = 128
SPAN = 64
SIDE = 4
CAP = 4
HEADS = 4
GROUPS = 16
WIDTH = HEADS * HEAD
OFFSET = (0, -1, 1, 2)
FAR = -1e30
SCORE = 1.4426950408889634 * HEAD**-0.5


def slot_table(core, shard_of, row_of, count_of):
    ring = lax.broadcasted_iota(jnp.int32, (8, 128), 0)
    lane = lax.broadcasted_iota(jnp.int32, (8, 128), 1)
    table = jnp.zeros((8, 128), jnp.int32)
    pairs = 2 * GROUPS
    owners = [shard_of[e % 2, e // 2] for e in range(pairs)]
    for e, owner in enumerate(owners):
        rank = jnp.int32(0)
        for other in owners[:e]:
            rank = rank + jnp.where(other == owner, 1, 0)
        down, across = owner // SIDE, owner % SIDE
        owner_a = down + core * (across - down)
        owner_b = across + core * (down - across)
        slot = owner_a * CAP + jnp.minimum(rank, CAP - 1)
        fits = jnp.where(rank < CAP, 0, 96)
        entry = jnp.where(lane == slot + fits, e // 2, 0)
        entry = entry + jnp.where(lane == 16 + slot + fits, row_of[e % 2, e // 2], 0)
        entry = entry + jnp.where(lane == 32 + e, slot, 0)
        if e % 2 == 0:
            used = jnp.int32(1)
        else:
            used = jnp.where(count_of[e // 2] > 1, 1, 0)
        entry = entry + jnp.where(lane == 64 + e, used, 0)
        table = table + jnp.where(ring == owner_b, entry, 0)
    return table


def kernel(
    hidden, wq, wo, kv, shard_of, row_of, count_of, out,
    hid_v, wq_v, w_all, kvs, qs, parts, lses, table, tab_v, tab_s, borrowed, sent, stats, opp, opp_stats,
    back, back_stats, ctx, carried, total, keep, give, got, ship, landed,
    hid_sem, load_sem, tab_sem, kv_sem, q_sem, t_sem, b_sem, c_sem, w_sem, r_sem, x_sem, g_sem, s_sem,
):
    seq = lax.axis_index("seq")
    tp = lax.axis_index("tp")
    core = tp % 2
    z = tp // 2
    row, col = seq // SIDE, seq % SIDE
    a = row + core * (col - row)
    b = col + core * (row - col)
    a_step, b_step = SIDE - 3 * core, 1 + 3 * core

    def along_a(by):
        return (lax.rem(a + by + SIDE, SIDE) * a_step + b * b_step, tp)

    def along_b(by):
        return (a * a_step + lax.rem(b + by + SIDE, SIDE) * b_step, tp)

    def along_z(by):
        return (seq, lax.rem(z + by + SIDE, SIDE) * 2 + core)

    sibling = (seq, z * 2 + 1 - core)
    next_block = (lax.rem(seq + 1, 16), tp)
    last_block = (lax.rem(seq + 15, 16), tp)

    def remote(src, dst, sems, at, device):
        return pltpu.make_async_remote_copy(
            src_ref=src,
            dst_ref=dst,
            send_sem=sems.at[(0, *at)],
            recv_sem=sems.at[(1, *at)],
            device_id=device,
            device_id_type=pl.DeviceIdType.MESH,
        )

    started = []

    def send(copy):
        copy.start()
        started.append(copy)

    def arrive(*copies):
        for copy in copies:
            copy.wait_recv()

    wq_load = pltpu.make_async_copy(wq, wq_v, load_sem.at[0])
    wq_load.start()
    hid_loads = [
        pltpu.make_async_copy(hidden.at[pl.ds(256 * c, 256), :], hid_v.at[c], hid_sem.at[c])
        for c in range(4)
    ]
    for copy in hid_loads:
        copy.start()
    lanes = [pl.ds(h * HEAD, HEAD) for h in range(HEADS)]
    kv_loads = [
        pltpu.make_async_copy(kv.at[:, :, :, lanes[h]], kvs[0][h], load_sem.at[1 + h])
        for h in range(HEADS)
    ]
    for copy in kv_loads:
        copy.start()

    def columns(of):
        return pl.ds(pl.multiple_of(of * 1024, 1024), 1024)

    w_load = pltpu.make_async_copy(wo.at[:, columns(z)], w_all.at[z], load_sem.at[5])
    w_load.start()

    barrier = pltpu.get_barrier_semaphore()
    friends = (
        along_a(1), along_a(-1), along_b(1), along_b(-1), along_z(1), along_z(-1), along_z(2),
        sibling, next_block, last_block,
    )
    for device in friends:
        pl.semaphore_signal(barrier, inc=1, device_id=device, device_id_type=pl.DeviceIdType.MESH)
    pl.semaphore_wait(barrier, len(friends))

    low, high = pl.ds(0, 4), pl.ds(4, 4)
    kv_copies = [
        [
            remote(kv.at[low, :, :, lanes[h]], kvs[1][h].at[low], kv_sem, (h, 0), along_a(1)),
            remote(kv.at[high, :, :, lanes[h]], kvs[2][h].at[high], kv_sem, (h, 1), along_a(-1)),
            remote(kv.at[high, :, :, lanes[h]], kvs[1][h].at[high], kv_sem, (h, 2), along_a(1)),
            remote(kv.at[low, :, :, lanes[h]], kvs[2][h].at[low], kv_sem, (h, 3), along_a(-1)),
            remote(kvs[1][h].at[low], kvs[3][h].at[low], kv_sem, (h, 4), along_a(1)),
            remote(kvs[2][h].at[high], kvs[3][h].at[high], kv_sem, (h, 5), along_a(-1)),
        ]
        for h in range(HEADS)
    ]
    tab_copies = [
        remote(table, tab_v.at[0], t_sem, (0,), along_b(1)),
        remote(table, tab_v.at[1], t_sem, (1,), along_b(-1)),
        remote(tab_v.at[0], tab_v.at[2], t_sem, (2,), along_b(1)),
    ]
    w_copies = [
        remote(wo.at[:, columns(lax.rem(z + by + SIDE, SIDE))], w_all.at[z], w_sem, (j,), along_z(by))
        for j, by in enumerate((1, -1, 2))
    ]
    for h in range(2):
        for copy in kv_copies[h][:4]:
            send(copy)
    table[...] = slot_table(core, shard_of, row_of, count_of)
    for copy in tab_copies[:2]:
        send(copy)
    tab_load = pltpu.make_async_copy(table, tab_s.at[0], tab_sem.at[0])
    tab_load.start()
    for copy in w_copies:
        send(copy)

    lo_g, hi_g = pl.ds(0, 8), pl.ds(8, 8)
    q_copies = [
        [
            remote(qs[0][h].at[lo_g], qs[1][h].at[lo_g], q_sem, (h, 0), along_b(1)),
            remote(qs[0][h].at[hi_g], qs[2][h].at[hi_g], q_sem, (h, 1), along_b(-1)),
            remote(qs[0][h].at[hi_g], qs[1][h].at[hi_g], q_sem, (h, 2), along_b(1)),
            remote(qs[0][h].at[lo_g], qs[2][h].at[lo_g], q_sem, (h, 3), along_b(-1)),
            remote(qs[1][h].at[lo_g], qs[3][h].at[lo_g], q_sem, (h, 4), along_b(1)),
            remote(qs[2][h].at[hi_g], qs[3][h].at[hi_g], q_sem, (h, 5), along_b(-1)),
        ]
        for h in range(HEADS)
    ]
    lend = remote(borrowed.at[0], borrowed.at[1], b_sem, (), last_block)
    wq_load.wait()
    tail = jnp.zeros((1, WIDTH), F32)
    first_row = lax.broadcasted_iota(jnp.int32, (256, WIDTH), 0) == 0
    for c in range(4):
        hid_loads[c].wait()
        square = jnp.zeros((256, HEAD), F32)
        for j in range(32):
            piece = hid_v[c, :, j * HEAD : (j + 1) * HEAD].astype(F32)
            square = square + piece * piece
        scale = lax.rsqrt(jnp.sum(square, axis=1, keepdims=True) * (1.0 / 4096) + 1e-05)
        cols = [
            jnp.dot(hid_v[c], wq_v[:, n * 256 : (n + 1) * 256], preferred_element_type=F32) * scale
            for n in range(2)
        ]
        queries = jnp.concatenate(cols, axis=1)
        moved = jnp.where(first_row, tail, pltpu.roll(queries, 1, 0))
        tail = queries[255:256]
        moved = moved.astype(BF16).reshape(4, SPAN, WIDTH)
        if c == 0:
            borrowed[0] = moved[0]
            send(lend)
        for h in range(HEADS):
            cut = slice(h * HEAD, (h + 1) * HEAD)
            if c == 0:
                qs[0][h][0:3] = moved[1:4, :, cut]
            else:
                qs[0][h][4 * c - 1 : 4 * c + 3] = moved[:, :, cut]
        if c == 2:
            send(q_copies[0][0])
            send(q_copies[0][3])
    arrive(lend)
    span_row = lax.broadcasted_iota(jnp.int32, (SPAN, HEAD), 0)
    for h in range(HEADS):
        cut = slice(h * HEAD, (h + 1) * HEAD)
        last = jnp.where(span_row == 0, tail[:, cut], borrowed[1, :, cut].astype(F32))
        qs[0][h][15] = last.astype(BF16)
    send(q_copies[0][1])
    send(q_copies[0][2])
    for copy in q_copies[1][:4]:
        send(copy)

    arrive(tab_copies[0])
    send(tab_copies[2])
    arrive(tab_copies[1], tab_copies[2])
    tab_loads = [
        pltpu.make_async_copy(tab_v.at[d], tab_s.at[d + 1], tab_sem.at[d + 1]) for d in range(3)
    ]
    for copy in tab_loads:
        copy.start()
    for copy in [tab_load, *tab_loads, *kv_loads]:
        copy.wait()

    lane = lax.broadcasted_iota(jnp.int32, (SPAN, HEAD), 1)

    def slots(h, d, i):
        base = lax.rem(a + OFFSET[i] + SIDE, SIDE) * CAP
        spots = [base + k for k in range(CAP)]
        values, scores = [], []
        for at in spots:
            query = qs[d][h][tab_s[d, b, at]]
            cached = tab_s[d, b, 16 + at]
            values.append(kvs[i][h][cached, 1])
            scores.append(
                lax.dot_general(
                    query,
                    kvs[i][h][cached, 0],
                    (((1,), (1,)), ((), ())),
                    preferred_element_type=F32,
                )
                * SCORE
            )
        highest = [jnp.max(score, axis=1, keepdims=True) for score in scores]
        expon = [jnp.exp2(score - high) for score, high in zip(scores, highest)]
        totals = [jnp.sum(one, axis=1, keepdims=True) for one in expon]
        for at, one, value, high, whole in zip(spots, expon, values, highest, totals):
            part = jnp.dot(one.astype(BF16), value, preferred_element_type=F32)
            parts[h % 2, d, at] = part * (1.0 / whole)
            lses[h % 2, d, at] = jnp.broadcast_to(high + jnp.log2(whole), (SPAN, HEAD))

    def merged(sources):
        top = functools.reduce(jnp.maximum, [lse for lse, _ in sources])
        shares = [jnp.exp2(lse - top) for lse, _ in sources]
        whole = functools.reduce(jnp.add, shares)
        mixed = functools.reduce(
            jnp.add, [share * part.astype(F32) for share, (_, part) in zip(shares, sources)]
        )
        return mixed * (1.0 / whole), top + jnp.log2(whole)

    def from_slots(h, d, g):
        found = []
        for n in range(2):
            at = tab_s[d, b, 32 + 2 * g + n]
            used = tab_s[d, b, 64 + 2 * g + n]
            lse = jnp.where(jnp.full((SPAN, HEAD), used, jnp.int32) > 0, lses[h % 2, d, at], FAR)
            found.append((lse, parts[h % 2, d, at]))
        return found

    def stats_of(held, g):
        turned = pltpu.roll(held, lax.rem(HEAD - g, HEAD), 1)
        return jnp.broadcast_to(turned[:, 0:1], (SPAN, HEAD))

    def contribute(h, d, first, last, extra, held):
        def one(g, held):
            sources = from_slots(h, d, g)
            if extra is not None:
                sources.append((stats_of(opp_stats[h, extra], g), opp[h, extra, g - first]))
            mixed, lse = merged(sources)
            sent[h, d - 1, g] = mixed.astype(BF16)
            return jnp.where(lane == g, lse, held)

        return lax.fori_loop(first, last, one, held, unroll=4)

    none = jnp.zeros((SPAN, HEAD), F32)
    opp_copies = [
        [
            remote(sent.at[h, 2, lo_g], opp.at[h, 0], r_sem, (h, 0), along_b(1)),
            remote(stats.at[h, 2], opp_stats.at[h, 0], r_sem, (h, 1), along_b(1)),
            remote(sent.at[h, 2, hi_g], opp.at[h, 1], r_sem, (h, 2), along_b(-1)),
            remote(stats.at[h, 2], opp_stats.at[h, 1], r_sem, (h, 3), along_b(-1)),
        ]
        for h in range(HEADS)
    ]
    back_copies = [
        [
            remote(sent.at[h, 1, hi_g], back.at[h, 0, hi_g], r_sem, (h, 4), along_b(1)),
            remote(sent.at[h, 1, lo_g], back.at[h, 0, lo_g], r_sem, (h, 5), along_b(1)),
            remote(stats.at[h, 1], back_stats.at[h, 0], r_sem, (h, 6), along_b(1)),
            remote(sent.at[h, 0, lo_g], back.at[h, 1, lo_g], r_sem, (h, 7), along_b(-1)),
            remote(sent.at[h, 0, hi_g], back.at[h, 1, hi_g], r_sem, (h, 8), along_b(-1)),
            remote(stats.at[h, 0], back_stats.at[h, 1], r_sem, (h, 9), along_b(-1)),
        ]
        for h in range(HEADS)
    ]
    carry_copies = [
        remote(carried.at[0, h], carried.at[1, h], c_sem, (h,), next_block) for h in range(HEADS)
    ]
    before, after = lax.rem(z + 3, SIDE), lax.rem(z + 1, SIDE)
    ctx_copies = [
        [
            remote(ctx.at[h, z, hi_g], ctx.at[h, z, hi_g], x_sem, (h, 0), along_z(-1)),
            remote(ctx.at[h, z, hi_g], ctx.at[h, z, hi_g], x_sem, (h, 1), along_z(1)),
            remote(ctx.at[h, z, lo_g], ctx.at[h, z, lo_g], x_sem, (h, 2), along_z(1)),
            remote(ctx.at[h, z, lo_g], ctx.at[h, z, lo_g], x_sem, (h, 3), along_z(-1)),
            remote(ctx.at[h, after, hi_g], ctx.at[h, after, hi_g], x_sem, (h, 4), along_z(-1)),
            remote(ctx.at[h, before, lo_g], ctx.at[h, before, lo_g], x_sem, (h, 5), along_z(1)),
        ]
        for h in range(HEADS)
    ]

    def pass_on(h):
        arrive(kv_copies[h][0])
        send(kv_copies[h][4])
        arrive(kv_copies[h][1])
        send(kv_copies[h][5])
        arrive(q_copies[h][0])
        send(q_copies[h][4])
        arrive(q_copies[h][1])
        send(q_copies[h][5])
        if h + 2 < HEADS:
            for copy in kv_copies[h + 2][:4] + q_copies[h + 2][:4]:
                send(copy)
        arrive(*kv_copies[h][2:4], *q_copies[h][2:4])

    def finish(h, g):
        sources = from_slots(h, 0, g)
        sources.append((stats_of(back_stats[h, 0], g), back[h, 0, g]))
        sources.append((stats_of(back_stats[h, 1], g), back[h, 1, g]))
        return merged(sources)[0]

    def early(h):
        for d in range(3):
            for i in range(3):
                slots(h, d, i)

    def late(h):
        arrive(*q_copies[h][4:6])
        for i in range(3):
            slots(h, 3, i)
        arrive(*kv_copies[h][4:6])
        slots(h, 3, 3)
        stats[h, 2] = contribute(h, 3, 0, GROUPS, None, none)
        for copy in opp_copies[h]:
            send(copy)
        slots(h, 2, 3)
        held_next = contribute(h, 2, 8, GROUPS, None, none)
        send(back_copies[h][0])
        slots(h, 1, 3)
        held_last = contribute(h, 1, 0, 8, None, none)
        send(back_copies[h][3])
        slots(h, 0, 3)
        return held_next, held_last

    def give_back(h, held_next, held_last):
        arrive(*opp_copies[h][0:2])
        stats[h, 1] = contribute(h, 2, 0, 8, 0, held_next)
        send(back_copies[h][1])
        send(back_copies[h][2])
        arrive(*opp_copies[h][2:4])
        stats[h, 0] = contribute(h, 1, 8, GROUPS, 1, held_last)
        send(back_copies[h][4])
        send(back_copies[h][5])

    head_rows = {}

    def context(h):
        arrive(*back_copies[h])
        mixed = finish(h, GROUPS - 1)
        carried[0, h] = pltpu.roll(mixed, SPAN - 1, 0).astype(BF16)
        send(carry_copies[h])

        def one_span(step, head_row):
            g = GROUPS - 2 - step
            mixed = finish(h, g)
            moved = jnp.where(span_row == SPAN - 1, head_row, pltpu.roll(mixed, SPAN - 1, 0))
            ctx[h, z, g + 1] = moved.astype(BF16)
            return mixed[0:1]

        head_row = lax.fori_loop(0, 8, one_span, mixed[0:1], unroll=4)
        send(ctx_copies[h][0])
        send(ctx_copies[h][1])
        head_rows[h] = lax.fori_loop(8, GROUPS - 1, one_span, head_row, unroll=7)

    def context_out(h):
        arrive(carry_copies[h])
        here = jnp.full((SPAN, HEAD), seq, jnp.int32) > 0
        arrived = jnp.where(here, carried[1, h].astype(F32), 0.0)
        ctx[h, z, 0] = jnp.where(span_row == SPAN - 1, head_rows[h], arrived).astype(BF16)
        send(ctx_copies[h][2])
        send(ctx_copies[h][3])

    def context_on(h):
        arrive(ctx_copies[h][0])
        send(ctx_copies[h][4])
        arrive(ctx_copies[h][2])
        send(ctx_copies[h][5])

    def product(h, at, n, chips):
        left = jnp.concatenate([ctx[h, j, at].reshape(-1, HEAD) for j in chips], axis=1)
        cut = pl.ds(pl.multiple_of(n * 256, 256), 256)
        right = jnp.concatenate(
            [w_all[j, h * HEAD : (h + 1) * HEAD, cut] for j in chips], axis=0
        )
        return jnp.dot(left, right, preferred_element_type=F32), cut

    def project(h):
        if h == 0:
            w_load.wait()
            arrive(*w_copies)
        arrive(ctx_copies[h][1], ctx_copies[h][3])
        chips = (z, before, after)
        if h + 1 < HEADS:
            arrive(*ctx_copies[h][4:])
            chips = range(SIDE)

        def one(step, carry):
            at = pl.ds((step // 4) * 4, 4)
            value, cut = product(h, at, step % 4, chips)
            value = value.reshape(4, SPAN, 256)
            total[at, :, cut] = value if h == 0 else total[at, :, cut] + value
            return carry

        lax.fori_loop(0, 16, one, 0)

    pass_on(0)
    held = [None] * HEADS
    for h in range(HEADS):
        early(h)
        if h + 1 < HEADS:
            pass_on(h + 1)
        if h >= 1:
            give_back(h - 1, *held[h - 1])
        if h >= 2:
            context_out(h - 2)
        held[h] = late(h)
        if h >= 1:
            context(h - 1)
        if h >= 2:
            context_on(h - 2)
        if h >= 3:
            project(h - 3)
    h = HEADS - 1
    give_back(h, *held[h])
    context_out(h - 1)
    project(h - 2)
    context(h)
    context_on(h - 1)
    context_out(h)
    project(h - 1)
    context_on(h)
    project(h)
    arrive(*ctx_copies[h][4:])

    ways = (2, 1, -1, 0)
    give_copies = [
        remote(give.at[j], got.at[j], g_sem, (j,), sibling) for j in range(SIDE)
    ]
    ship_copies = [
        remote(ship.at[j], landed.at[j], s_sem, (j,), along_z(by)) for j, by in enumerate(ways[:3])
    ]
    for j, by in enumerate(ways):
        first = lax.rem(z + by + SIDE, SIDE) * 4
        for whose, to in ((1 - core, give), (core, keep)):
            at = pl.ds(first + 2 * whose, 2)

            def one(n, carry, at=at, to=to, j=j):
                value, cut = product(h, at, n, (lax.rem(z + 2, SIDE),))
                value = value + total[at, :, cut].reshape(128, 256)
                to[j, :, cut] = value.astype(to.dtype)
                return carry

            lax.fori_loop(0, 4, one, 0)
            if to is give:
                send(give_copies[j])
    for j, by in enumerate(ways):
        arrive(give_copies[j])
        value = (keep[j] + got[j].astype(F32)).astype(BF16)
        if by == 0:
            out[:, columns(z)] = value
        else:
            ship[j] = value
            send(ship_copies[j])
    for copy in started[:-3]:
        copy.wait_send()
    for j in (1, 2, 0):
        arrive(ship_copies[j])
        out[:, columns(lax.rem(z - ways[j] + SIDE, SIDE))] = landed[j]
    for copy in started[-3:]:
        copy.wait_send()


def shards(hidden, query_weight, out_weight, kv_cache, nbr_shard, nbr_row, nbr_count):
    dma = pltpu.SemaphoreType.DMA
    hbm = pl.BlockSpec(memory_space=pl.ANY)
    return pl.pallas_call(
        kernel,
        out_shape=jax.ShapeDtypeStruct((128, 4096), BF16),
        in_specs=[hbm] * 4 + [pl.BlockSpec(memory_space=pltpu.SMEM)] * 3,
        out_specs=pl.BlockSpec(memory_space=pltpu.VMEM),
        scratch_shapes=[
            pltpu.VMEM((4, 256, 4096), BF16),
            pltpu.VMEM((4096, WIDTH), BF16),
            pltpu.VMEM((SIDE, WIDTH, 1024), BF16),
            [[pltpu.VMEM((8, 2, 128, HEAD), BF16)] * HEADS] * SIDE,
            [[pltpu.VMEM((GROUPS, SPAN, HEAD), BF16)] * HEADS] * SIDE,
            pltpu.VMEM((2, SIDE, 16, SPAN, HEAD), F32),
            pltpu.VMEM((2, SIDE, 16, SPAN, HEAD), F32),
            pltpu.VMEM((8, 128), jnp.int32),
            pltpu.VMEM((3, 8, 128), jnp.int32),
            pltpu.SMEM((4, 8, 128), jnp.int32),
            pltpu.VMEM((2, SPAN, WIDTH), BF16),
            pltpu.VMEM((HEADS, 3, GROUPS, SPAN, HEAD), BF16),
            pltpu.VMEM((HEADS, 3, SPAN, HEAD), F32),
            pltpu.VMEM((HEADS, 2, 8, SPAN, HEAD), BF16),
            pltpu.VMEM((HEADS, 2, SPAN, HEAD), F32),
            pltpu.VMEM((HEADS, 2, GROUPS, SPAN, HEAD), BF16),
            pltpu.VMEM((HEADS, 2, SPAN, HEAD), F32),
            pltpu.VMEM((HEADS, SIDE, GROUPS, SPAN, HEAD), BF16),
            pltpu.VMEM((2, HEADS, SPAN, HEAD), BF16),
            pltpu.VMEM((GROUPS, SPAN, 1024), F32),
            pltpu.VMEM((SIDE, 128, 1024), F32),
            pltpu.VMEM((SIDE, 128, 1024), BF16),
            pltpu.VMEM((SIDE, 128, 1024), BF16),
            pltpu.VMEM((3, 128, 1024), BF16),
            pltpu.VMEM((3, 128, 1024), BF16),
            dma((4,)),
            dma((6,)),
            dma((4,)),
            dma((2, HEADS, 6)),
            dma((2, HEADS, 6)),
            dma((2, 3)),
            dma((2,)),
            dma((2, HEADS)),
            dma((2, 3)),
            dma((2, HEADS, 10)),
            dma((2, HEADS, 6)),
            dma((2, SIDE)),
            dma((2, 3)),
        ],
        compiler_params=pltpu.CompilerParams(
            collective_id=0, has_side_effects=True, vmem_limit_bytes=62 * 1024 * 1024
        ),
        cost_estimate=pl.CostEstimate(flops=9_000_000_000, bytes_accessed=20_000_000, transcendentals=2_000_000),
    )(hidden, query_weight, out_weight, kv_cache, nbr_shard.T, nbr_row.T, nbr_count)


def solution(mesh):
    placed = (
        P("seq", None),
        P(None, "tp"),
        P("tp", None),
        P("seq", None, None, "tp"),
        P("seq", None),
        P("seq", None),
        P("seq"),
    )
    return jax.shard_map(
        shards, mesh=mesh, in_specs=placed, out_specs=P(("seq", "tp"), None), check_vma=False
    )
```

```python
import functools

import jax
import jax.numpy as jnp
from jax import lax
from jax.experimental import pallas as pl
from jax.experimental.pallas import tpu as pltpu
from jax.sharding import PartitionSpec as P

F32 = jnp.float32
BF16 = jnp.bfloat16
HEAD = 128
SPAN = 64
SIDE = 4
CAP = 4
HEADS = 4
GROUPS = 16
WIDTH = HEADS * HEAD
OFFSET = (0, -1, 1, 2)
FAR = -1e30
SCORE = 1.4426950408889634 * HEAD**-0.5


def slot_table(core, shard_of, row_of, count_of):
    ring = lax.broadcasted_iota(jnp.int32, (8, 128), 0)
    lane = lax.broadcasted_iota(jnp.int32, (8, 128), 1)
    table = jnp.zeros((8, 128), jnp.int32)
    pairs = 2 * GROUPS
    owners = [shard_of[e % 2, e // 2] for e in range(pairs)]
    for e, owner in enumerate(owners):
        rank = jnp.int32(0)
        for other in owners[:e]:
            rank = rank + jnp.where(other == owner, 1, 0)
        down, across = owner // SIDE, owner % SIDE
        owner_a = down + core * (across - down)
        owner_b = across + core * (down - across)
        slot = owner_a * CAP + jnp.minimum(rank, CAP - 1)
        fits = jnp.where(rank < CAP, 0, 96)
        entry = jnp.where(lane == slot + fits, e // 2, 0)
        entry = entry + jnp.where(lane == 16 + slot + fits, row_of[e % 2, e // 2], 0)
        entry = entry + jnp.where(lane == 32 + e, slot, 0)
        if e % 2 == 0:
            used = jnp.int32(1)
        else:
            used = jnp.where(count_of[e // 2] > 1, 1, 0)
        entry = entry + jnp.where(lane == 64 + e, used, 0)
        table = table + jnp.where(ring == owner_b, entry, 0)
    return table


def kernel(
    hidden, wq, wo, kv, shard_of, row_of, count_of, out,
    hid_v, wq_v, w_all, kvs, qs, parts, lses, table, tab_v, tab_s, borrowed, sent, stats, opp, opp_stats,
    back, back_stats, ctx, carried, total, keep, give, got, ship, landed,
    hid_sem, load_sem, tab_sem, kv_sem, q_sem, t_sem, b_sem, c_sem, w_sem, r_sem, x_sem, g_sem, s_sem,
):
    seq = lax.axis_index("seq")
    tp = lax.axis_index("tp")
    core = tp % 2
    z = tp // 2
    row, col = seq // SIDE, seq % SIDE
    a = row + core * (col - row)
    b = col + core * (row - col)
    a_step, b_step = SIDE - 3 * core, 1 + 3 * core

    def along_a(by):
        return (lax.rem(a + by + SIDE, SIDE) * a_step + b * b_step, tp)

    def along_b(by):
        return (a * a_step + lax.rem(b + by + SIDE, SIDE) * b_step, tp)

    def along_z(by):
        return (seq, lax.rem(z + by + SIDE, SIDE) * 2 + core)

    sibling = (seq, z * 2 + 1 - core)
    next_block = (lax.rem(seq + 1, 16), tp)
    last_block = (lax.rem(seq + 15, 16), tp)

    def remote(src, dst, sems, at, device):
        return pltpu.make_async_remote_copy(
            src_ref=src,
            dst_ref=dst,
            send_sem=sems.at[(0, *at)],
            recv_sem=sems.at[(1, *at)],
            device_id=device,
            device_id_type=pl.DeviceIdType.MESH,
        )

    started = []

    def send(copy):
        copy.start()
        started.append(copy)

    def arrive(*copies):
        for copy in copies:
            copy.wait_recv()

    wq_load = pltpu.make_async_copy(wq, wq_v, load_sem.at[0])
    wq_load.start()
    hid_loads = [
        pltpu.make_async_copy(hidden.at[pl.ds(256 * c, 256), :], hid_v.at[c], hid_sem.at[c])
        for c in range(4)
    ]
    for copy in hid_loads:
        copy.start()
    lanes = [pl.ds(h * HEAD, HEAD) for h in range(HEADS)]
    kv_loads = [
        pltpu.make_async_copy(kv.at[:, :, :, lanes[h]], kvs[0][h], load_sem.at[1 + h])
        for h in range(HEADS)
    ]
    for copy in kv_loads:
        copy.start()

    def columns(of):
        return pl.ds(pl.multiple_of(of * 1024, 1024), 1024)

    w_load = pltpu.make_async_copy(wo.at[:, columns(z)], w_all.at[z], load_sem.at[5])
    w_load.start()

    barrier = pltpu.get_barrier_semaphore()
    friends = (
        along_a(1), along_a(-1), along_b(1), along_b(-1), along_z(1), along_z(-1), along_z(2),
        sibling, next_block, last_block,
    )
    for device in friends:
        pl.semaphore_signal(barrier, inc=1, device_id=device, device_id_type=pl.DeviceIdType.MESH)
    pl.semaphore_wait(barrier, len(friends))

    low, high = pl.ds(0, 4), pl.ds(4, 4)
    kv_copies = [
        [
            remote(kv.at[low, :, :, lanes[h]], kvs[1][h].at[low], kv_sem, (h, 0), along_a(1)),
            remote(kv.at[high, :, :, lanes[h]], kvs[2][h].at[high], kv_sem, (h, 1), along_a(-1)),
            remote(kv.at[high, :, :, lanes[h]], kvs[1][h].at[high], kv_sem, (h, 2), along_a(1)),
            remote(kv.at[low, :, :, lanes[h]], kvs[2][h].at[low], kv_sem, (h, 3), along_a(-1)),
            remote(kvs[1][h].at[low], kvs[3][h].at[low], kv_sem, (h, 4), along_a(1)),
            remote(kvs[2][h].at[high], kvs[3][h].at[high], kv_sem, (h, 5), along_a(-1)),
        ]
        for h in range(HEADS)
    ]
    tab_copies = [
        remote(table, tab_v.at[0], t_sem, (0,), along_b(1)),
        remote(table, tab_v.at[1], t_sem, (1,), along_b(-1)),
        remote(tab_v.at[0], tab_v.at[2], t_sem, (2,), along_b(1)),
    ]
    w_copies = [
        remote(wo.at[:, columns(lax.rem(z + by + SIDE, SIDE))], w_all.at[z], w_sem, (j,), along_z(by))
        for j, by in enumerate((1, -1, 2))
    ]
    for h in range(2):
        for copy in kv_copies[h][:4]:
            send(copy)
    table[...] = slot_table(core, shard_of, row_of, count_of)
    for copy in tab_copies[:2]:
        send(copy)
    tab_load = pltpu.make_async_copy(table, tab_s.at[0], tab_sem.at[0])
    tab_load.start()
    for copy in w_copies:
        send(copy)

    lo_g, hi_g = pl.ds(0, 8), pl.ds(8, 8)
    q_copies = [
        [
            remote(qs[0][h].at[lo_g], qs[1][h].at[lo_g], q_sem, (h, 0), along_b(1)),
            remote(qs[0][h].at[hi_g], qs[2][h].at[hi_g], q_sem, (h, 1), along_b(-1)),
            remote(qs[0][h].at[hi_g], qs[1][h].at[hi_g], q_sem, (h, 2), along_b(1)),
            remote(qs[0][h].at[lo_g], qs[2][h].at[lo_g], q_sem, (h, 3), along_b(-1)),
            remote(qs[1][h].at[lo_g], qs[3][h].at[lo_g], q_sem, (h, 4), along_b(1)),
            remote(qs[2][h].at[hi_g], qs[3][h].at[hi_g], q_sem, (h, 5), along_b(-1)),
        ]
        for h in range(HEADS)
    ]
    lend = remote(borrowed.at[0], borrowed.at[1], b_sem, (), last_block)
    wq_load.wait()
    tail = jnp.zeros((1, WIDTH), F32)
    first_row = lax.broadcasted_iota(jnp.int32, (256, WIDTH), 0) == 0
    for c in range(4):
        hid_loads[c].wait()
        square = jnp.zeros((256, HEAD), F32)
        for j in range(32):
            piece = hid_v[c, :, j * HEAD : (j + 1) * HEAD].astype(F32)
            square = square + piece * piece
        scale = lax.rsqrt(jnp.sum(square, axis=1, keepdims=True) * (1.0 / 4096) + 1e-05)
        cols = [
            jnp.dot(hid_v[c], wq_v[:, n * 256 : (n + 1) * 256], preferred_element_type=F32) * scale
            for n in range(2)
        ]
        queries = jnp.concatenate(cols, axis=1)
        moved = jnp.where(first_row, tail, pltpu.roll(queries, 1, 0))
        tail = queries[255:256]
        moved = moved.astype(BF16).reshape(4, SPAN, WIDTH)
        if c == 0:
            borrowed[0] = moved[0]
            send(lend)
        for h in range(HEADS):
            cut = slice(h * HEAD, (h + 1) * HEAD)
            if c == 0:
                qs[0][h][0:3] = moved[1:4, :, cut]
            else:
                qs[0][h][4 * c - 1 : 4 * c + 3] = moved[:, :, cut]
        if c == 1:
            arrive(tab_copies[0])
            send(tab_copies[2])
        if c == 2:
            send(q_copies[0][0])
            send(q_copies[0][3])
    arrive(lend)
    span_row = lax.broadcasted_iota(jnp.int32, (SPAN, HEAD), 0)
    for h in range(HEADS):
        cut = slice(h * HEAD, (h + 1) * HEAD)
        last = jnp.where(span_row == 0, tail[:, cut], borrowed[1, :, cut].astype(F32))
        qs[0][h][15] = last.astype(BF16)
    send(q_copies[0][1])
    send(q_copies[0][2])
    for copy in q_copies[1][:4]:
        send(copy)

    lane = lax.broadcasted_iota(jnp.int32, (SPAN, HEAD), 1)

    def slots(h, d, i):
        base = lax.rem(a + OFFSET[i] + SIDE, SIDE) * CAP
        spots = [base + k for k in range(CAP)]
        values, scores = [], []
        for at in spots:
            query = qs[d][h][tab_s[d, b, at]]
            cached = tab_s[d, b, 16 + at]
            values.append(kvs[i][h][cached, 1])
            scores.append(
                lax.dot_general(
                    query,
                    kvs[i][h][cached, 0],
                    (((1,), (1,)), ((), ())),
                    preferred_element_type=F32,
                )
                * SCORE
            )
        highest = [jnp.max(score, axis=1, keepdims=True) for score in scores]
        expon = [jnp.exp2(score - high) for score, high in zip(scores, highest)]
        totals = [jnp.sum(one, axis=1, keepdims=True) for one in expon]
        for at, one, value, high, whole in zip(spots, expon, values, highest, totals):
            part = jnp.dot(one.astype(BF16), value, preferred_element_type=F32)
            parts[h % 2, d, at] = part * (1.0 / whole)
            lses[h % 2, d, at] = jnp.broadcast_to(high + jnp.log2(whole), (SPAN, HEAD))

    def merged(sources):
        top = functools.reduce(jnp.maximum, [lse for lse, _ in sources])
        shares = [jnp.exp2(lse - top) for lse, _ in sources]
        whole = functools.reduce(jnp.add, shares)
        mixed = functools.reduce(
            jnp.add, [share * part.astype(F32) for share, (_, part) in zip(shares, sources)]
        )
        return mixed * (1.0 / whole), top + jnp.log2(whole)

    def from_slots(h, d, g):
        found = []
        for n in range(2):
            at = tab_s[d, b, 32 + 2 * g + n]
            used = tab_s[d, b, 64 + 2 * g + n]
            lse = jnp.where(jnp.full((SPAN, HEAD), used, jnp.int32) > 0, lses[h % 2, d, at], FAR)
            found.append((lse, parts[h % 2, d, at]))
        return found

    def stats_of(held, g):
        turned = pltpu.roll(held, lax.rem(HEAD - g, HEAD), 1)
        return jnp.broadcast_to(turned[:, 0:1], (SPAN, HEAD))

    def contribute(h, d, first, last, extra, held):
        def one(g, held):
            sources = from_slots(h, d, g)
            if extra is not None:
                sources.append((stats_of(opp_stats[h, extra], g), opp[h, extra, g - first]))
            mixed, lse = merged(sources)
            sent[h, d - 1, g] = mixed.astype(BF16)
            return jnp.where(lane == g, lse, held)

        return lax.fori_loop(first, last, one, held, unroll=4)

    none = jnp.zeros((SPAN, HEAD), F32)
    opp_copies = [
        [
            remote(sent.at[h, 2, lo_g], opp.at[h, 0], r_sem, (h, 0), along_b(1)),
            remote(stats.at[h, 2], opp_stats.at[h, 0], r_sem, (h, 1), along_b(1)),
            remote(sent.at[h, 2, hi_g], opp.at[h, 1], r_sem, (h, 2), along_b(-1)),
            remote(stats.at[h, 3], opp_stats.at[h, 1], r_sem, (h, 3), along_b(-1)),
        ]
        for h in range(HEADS)
    ]
    back_copies = [
        [
            remote(sent.at[h, 1, hi_g], back.at[h, 0, hi_g], r_sem, (h, 4), along_b(1)),
            remote(sent.at[h, 1, lo_g], back.at[h, 0, lo_g], r_sem, (h, 5), along_b(1)),
            remote(stats.at[h, 1], back_stats.at[h, 0], r_sem, (h, 6), along_b(1)),
            remote(sent.at[h, 0, lo_g], back.at[h, 1, lo_g], r_sem, (h, 7), along_b(-1)),
            remote(sent.at[h, 0, hi_g], back.at[h, 1, hi_g], r_sem, (h, 8), along_b(-1)),
            remote(stats.at[h, 0], back_stats.at[h, 1], r_sem, (h, 9), along_b(-1)),
        ]
        for h in range(HEADS)
    ]
    carry_copies = [
        remote(carried.at[0, h], carried.at[1, h], c_sem, (h,), next_block) for h in range(HEADS)
    ]
    before, after = lax.rem(z + 3, SIDE), lax.rem(z + 1, SIDE)
    ctx_copies = [
        [
            remote(ctx.at[h, z, hi_g], ctx.at[h, z, hi_g], x_sem, (h, 0), along_z(-1)),
            remote(ctx.at[h, z, hi_g], ctx.at[h, z, hi_g], x_sem, (h, 1), along_z(1)),
            remote(ctx.at[h, z, lo_g], ctx.at[h, z, lo_g], x_sem, (h, 2), along_z(1)),
            remote(ctx.at[h, z, lo_g], ctx.at[h, z, lo_g], x_sem, (h, 3), along_z(-1)),
            remote(ctx.at[h, after, hi_g], ctx.at[h, after, hi_g], x_sem, (h, 4), along_z(-1)),
            remote(ctx.at[h, before, lo_g], ctx.at[h, before, lo_g], x_sem, (h, 5), along_z(1)),
        ]
        for h in range(HEADS)
    ]

    def pass_on(h):
        arrive(kv_copies[h][0])
        send(kv_copies[h][4])
        arrive(kv_copies[h][1])
        send(kv_copies[h][5])
        arrive(q_copies[h][0])
        send(q_copies[h][4])
        arrive(q_copies[h][1])
        send(q_copies[h][5])
        if h + 2 < HEADS:
            for copy in kv_copies[h + 2][:4] + q_copies[h + 2][:4]:
                send(copy)
        arrive(*kv_copies[h][2:4], *q_copies[h][2:4])

    def finish(h, g):
        sources = from_slots(h, 0, g)
        sources.append((stats_of(back_stats[h, 0], g), back[h, 0, g]))
        sources.append((stats_of(back_stats[h, 1], g), back[h, 1, g]))
        return merged(sources)[0]

    def early(h):
        for d in range(3):
            for i in range(3):
                slots(h, d, i)

    def late(h):
        arrive(*q_copies[h][4:6])
        for i in range(3):
            slots(h, 3, i)
        arrive(*kv_copies[h][4:6])
        slots(h, 3, 3)
        for way in range(2):
            stats[h, 2 + way] = contribute(h, 3, 8 * way, 8 * way + 8, None, none)
            send(opp_copies[h][2 * way])
            send(opp_copies[h][2 * way + 1])
        slots(h, 2, 3)
        held_next = contribute(h, 2, 8, GROUPS, None, none)
        send(back_copies[h][0])
        slots(h, 1, 3)
        held_last = contribute(h, 1, 0, 8, None, none)
        send(back_copies[h][3])
        slots(h, 0, 3)
        return held_next, held_last

    def give_back(h, held_next, held_last):
        arrive(*opp_copies[h][0:2])
        stats[h, 1] = contribute(h, 2, 0, 8, 0, held_next)
        send(back_copies[h][1])
        send(back_copies[h][2])
        arrive(*opp_copies[h][2:4])
        stats[h, 0] = contribute(h, 1, 8, GROUPS, 1, held_last)
        send(back_copies[h][4])
        send(back_copies[h][5])

    head_rows = {}

    def context(h):
        arrive(*back_copies[h])
        mixed = finish(h, GROUPS - 1)
        carried[0, h] = pltpu.roll(mixed, SPAN - 1, 0).astype(BF16)
        send(carry_copies[h])

        def one_span(step, head_row):
            g = GROUPS - 2 - step
            mixed = finish(h, g)
            moved = jnp.where(span_row == SPAN - 1, head_row, pltpu.roll(mixed, SPAN - 1, 0))
            ctx[h, z, g + 1] = moved.astype(BF16)
            return mixed[0:1]

        head_row = lax.fori_loop(0, 8, one_span, mixed[0:1], unroll=4)
        send(ctx_copies[h][0])
        send(ctx_copies[h][1])
        head_rows[h] = lax.fori_loop(8, GROUPS - 1, one_span, head_row, unroll=7)

    def context_out(h):
        arrive(carry_copies[h])
        here = jnp.full((SPAN, HEAD), seq, jnp.int32) > 0
        arrived = jnp.where(here, carried[1, h].astype(F32), 0.0)
        ctx[h, z, 0] = jnp.where(span_row == SPAN - 1, head_rows[h], arrived).astype(BF16)
        send(ctx_copies[h][2])
        send(ctx_copies[h][3])

    def context_on(h):
        arrive(ctx_copies[h][0])
        send(ctx_copies[h][4])
        arrive(ctx_copies[h][2])
        send(ctx_copies[h][5])

    def product(h, at, n, chips):
        left = jnp.concatenate([ctx[h, j, at].reshape(-1, HEAD) for j in chips], axis=1)
        cut = pl.ds(pl.multiple_of(n * 256, 256), 256)
        right = jnp.concatenate(
            [w_all[j, h * HEAD : (h + 1) * HEAD, cut] for j in chips], axis=0
        )
        return jnp.dot(left, right, preferred_element_type=F32), cut

    def project(h):
        if h == 0:
            w_load.wait()
            arrive(*w_copies)
        arrive(ctx_copies[h][1], ctx_copies[h][3])
        chips = (z, before, after)
        if h + 1 < HEADS:
            arrive(*ctx_copies[h][4:])
            chips = range(SIDE)

        def one(step, carry):
            at = pl.ds((step // 4) * 4, 4)
            value, cut = product(h, at, step % 4, chips)
            value = value.reshape(4, SPAN, 256)
            total[at, :, cut] = value if h == 0 else total[at, :, cut] + value
            return carry

        lax.fori_loop(0, 16, one, 0)

    pass_on(0)

    arrive(tab_copies[1], tab_copies[2])
    tab_loads = [
        pltpu.make_async_copy(tab_v.at[d], tab_s.at[d + 1], tab_sem.at[d + 1]) for d in range(3)
    ]
    for copy in tab_loads:
        copy.start()
    for copy in [tab_load, *tab_loads, *kv_loads]:
        copy.wait()

    held = [None] * HEADS
    for h in range(HEADS):
        early(h)
        if h + 1 < HEADS:
            pass_on(h + 1)
        if h >= 1:
            give_back(h - 1, *held[h - 1])
        if h >= 2:
            context_out(h - 2)
        held[h] = late(h)
        if h >= 1:
            context(h - 1)
        if h >= 2:
            context_on(h - 2)
        if h >= 3:
            project(h - 3)
    h = HEADS - 1
    give_back(h, *held[h])
    context_out(h - 1)
    project(h - 2)
    context(h)
    context_on(h - 1)
    context_out(h)
    project(h - 1)
    context_on(h)
    project(h)
    arrive(*ctx_copies[h][4:])

    ways = (2, 1, -1, 0)
    give_copies = [
        remote(give.at[j], got.at[j], g_sem, (j,), sibling) for j in range(SIDE)
    ]
    ship_copies = [
        remote(ship.at[j], landed.at[j], s_sem, (j,), along_z(by)) for j, by in enumerate(ways[:3])
    ]
    for j, by in enumerate(ways):
        first = lax.rem(z + by + SIDE, SIDE) * 4
        for whose, to in ((1 - core, give), (core, keep)):
            at = pl.ds(first + 2 * whose, 2)

            def one(n, carry, at=at, to=to, j=j):
                value, cut = product(h, at, n, (lax.rem(z + 2, SIDE),))
                value = value + total[at, :, cut].reshape(128, 256)
                to[j, :, cut] = value.astype(to.dtype)
                return carry

            lax.fori_loop(0, 4, one, 0)
            if to is give:
                send(give_copies[j])
    for j, by in enumerate(ways):
        arrive(give_copies[j])
        value = (keep[j] + got[j].astype(F32)).astype(BF16)
        if by == 0:
            out[:, columns(z)] = value
        else:
            ship[j] = value
            send(ship_copies[j])
    for copy in started[:-3]:
        copy.wait_send()
    for j in (1, 2, 0):
        arrive(ship_copies[j])
        out[:, columns(lax.rem(z - ways[j] + SIDE, SIDE))] = landed[j]
    for copy in started[-3:]:
        copy.wait_send()


def shards(hidden, query_weight, out_weight, kv_cache, nbr_shard, nbr_row, nbr_count):
    dma = pltpu.SemaphoreType.DMA
    hbm = pl.BlockSpec(memory_space=pl.ANY)
    return pl.pallas_call(
        kernel,
        out_shape=jax.ShapeDtypeStruct((128, 4096), BF16),
        in_specs=[hbm] * 4 + [pl.BlockSpec(memory_space=pltpu.SMEM)] * 3,
        out_specs=pl.BlockSpec(memory_space=pltpu.VMEM),
        scratch_shapes=[
            pltpu.VMEM((4, 256, 4096), BF16),
            pltpu.VMEM((4096, WIDTH), BF16),
            pltpu.VMEM((SIDE, WIDTH, 1024), BF16),
            [[pltpu.VMEM((8, 2, 128, HEAD), BF16)] * HEADS] * SIDE,
            [[pltpu.VMEM((GROUPS, SPAN, HEAD), BF16)] * HEADS] * SIDE,
            pltpu.VMEM((2, SIDE, 16, SPAN, HEAD), F32),
            pltpu.VMEM((2, SIDE, 16, SPAN, HEAD), F32),
            pltpu.VMEM((8, 128), jnp.int32),
            pltpu.VMEM((3, 8, 128), jnp.int32),
            pltpu.SMEM((4, 8, 128), jnp.int32),
            pltpu.VMEM((2, SPAN, WIDTH), BF16),
            pltpu.VMEM((HEADS, 3, GROUPS, SPAN, HEAD), BF16),
            pltpu.VMEM((HEADS, 4, SPAN, HEAD), F32),
            pltpu.VMEM((HEADS, 2, 8, SPAN, HEAD), BF16),
            pltpu.VMEM((HEADS, 2, SPAN, HEAD), F32),
            pltpu.VMEM((HEADS, 2, GROUPS, SPAN, HEAD), BF16),
            pltpu.VMEM((HEADS, 2, SPAN, HEAD), F32),
            pltpu.VMEM((HEADS, SIDE, GROUPS, SPAN, HEAD), BF16),
            pltpu.VMEM((2, HEADS, SPAN, HEAD), BF16),
            pltpu.VMEM((GROUPS, SPAN, 1024), F32),
            pltpu.VMEM((SIDE, 128, 1024), F32),
            pltpu.VMEM((SIDE, 128, 1024), BF16),
            pltpu.VMEM((SIDE, 128, 1024), BF16),
            pltpu.VMEM((3, 128, 1024), BF16),
            pltpu.VMEM((3, 128, 1024), BF16),
            dma((4,)),
            dma((6,)),
            dma((4,)),
            dma((2, HEADS, 6)),
            dma((2, HEADS, 6)),
            dma((2, 3)),
            dma((2,)),
            dma((2, HEADS)),
            dma((2, 3)),
            dma((2, HEADS, 10)),
            dma((2, HEADS, 6)),
            dma((2, SIDE)),
            dma((2, 3)),
        ],
        compiler_params=pltpu.CompilerParams(
            collective_id=0, has_side_effects=True, vmem_limit_bytes=62 * 1024 * 1024
        ),
        cost_estimate=pl.CostEstimate(flops=9_000_000_000, bytes_accessed=20_000_000, transcendentals=2_000_000),
    )(hidden, query_weight, out_weight, kv_cache, nbr_shard.T, nbr_row.T, nbr_count)


def solution(mesh):
    placed = (
        P("seq", None),
        P(None, "tp"),
        P("tp", None),
        P("seq", None, None, "tp"),
        P("seq", None),
        P("seq", None),
        P("seq"),
    )
    return jax.shard_map(
        shards, mesh=mesh, in_specs=placed, out_specs=P(("seq", "tp"), None), check_vma=False
    )
```
